32 devices in a mesh: tile: 8 (over z, y), band: 4 (over x, core).
Axes of the slice: x: 2, y: 2, z: 4, core: 2. Of those that a mesh axis runs over, the one named last changes fastest.
Arguments:
- sky_model: bfloat16 [4, 16384, 128], P('band', 'tile'), may hold values from -6 to 6
- observed: bfloat16 [4, 8, 1024, 128], P('band', 'tile'), may hold values from -6 to 6
- row_weight: float32 [4, 8, 128], P('band', 'tile'), may hold values from 0.1 to 1
- foot_owner: int32 [4, 8, 1024, 1], P('band', 'tile'), may hold values from 0 to 7; in each aligned block of 1024 rows (0 to 1023, 1024 to 2047, ..., all dimensions but the last counted through in order) at most 256 rows name the same one
- foot_local: int32 [4, 8, 1024], P('band', 'tile'), may hold values from 0 to 2047
- row_offset: int32 [4, 8], P('band', 'tile'), may hold values from -4 to 4
- exposure_of: int32 [4, 8], P('band', 'tile'), may hold values from 0 to 255
- amplitude: float32 [4, 256], replicated, may hold values from 0.25 to 1
- subpixel_shift: float32 [256], replicated, may hold values from 0.05 to 0.95
- column_profile: float32 [256, 4, 25], replicated, may hold values from 0.05 to 0.3
- row_profile: float32 [256, 4, 25], replicated, may hold values from 0.05 to 0.3
Outputs:
- grad_sky: float32 [4, 16384, 128], P('band', 'tile')
- grad_params: float32 [5, 256], replicated
The draws below stay inside these ranges and needn't reach their ends.
Inputs may be any that keep to these rules, and one draw needn't show every extreme that they name: `foot_owner`: in each aligned block of 1024 columns (the columns of one device's row blocks) no owner index appears more than 256 times, and some owner appears exactly 256 times in some blocks.
All inputs are finite; a program needn't handle non-finite values.
Results may differ from the reference program's by a relative error of at most 0.006.
Values may be sent and summed in bfloat16 or wider, within the bound.
A program may use at most 64 MiB of HBM per device.

```python
import math
import jax
import jax.numpy as jnp
import numpy as np
from jax import lax

COLS = 1024
BLOCK_ROWS = 128
TAPS = 25
COMPS = 4
EXPO = 256
RB_DEV = 1
SEG_DEV = 2048
NSTRIP = 4
NRB = 8
NSEG = 16384
CAP = 256
N_TILE = 8


def plant(values, own_key, smallest, high):
    longest = values.shape.index(max(values.shape))
    spots = []
    for shift in (0, 1):
        where = [jax.random.randint(jax.random.fold_in(own_key, axis), (), 0, length) for axis, length in enumerate(values.shape)]
        where[longest] = (where[longest] + shift) % values.shape[longest]
        spots.append(tuple(where))
    return values.at[spots[0]].set(smallest).at[spots[1]].set(high)


def levels(key, dims, shards, least, top_value):
    gain = 1.0
    for dim, shards_of in shards:
        draws = jax.random.uniform(jax.random.fold_in(jax.random.fold_in(key, 6), dim), (shards_of,), jnp.float32, least / len(shards), top_value / len(shards))
        gain = gain * jnp.repeat(jnp.exp(draws), dims[dim] // shards_of).reshape((-1,) + (1,) * (len(dims) - 1 - dim))
    return gain


def assign_block(key, own, number, rows, amount, top, limit, lean):
    order = jax.random.permutation(key, amount)
    crowded, ordinary = portions_of(amount, rows * top, limit, lean, True), portions_of(amount, rows * top, limit, lean, False)
    places = jnp.arange(amount)

    def named(tallies, turn):
        used = int((tallies > 0).sum())
        fixed = max(1, used // 4)
        passed = fixed + (places - fixed + turn * (used - fixed)) % max(1, amount - fixed)
        return jnp.zeros((amount,), jnp.int32).at[order[jnp.where(places < fixed, places, passed)]].set(jnp.asarray(tallies, jnp.int32))

    tallies = jnp.where(number % 4 == 0, named(crowded, number // 4), named(ordinary, number - number // 4 - 1))
    mixed = jax.random.permutation(jax.random.fold_in(own, 3), amount)
    donor, taker = mixed[0:amount // 2 * 2:2], mixed[1:amount // 2 * 2:2]
    room = jnp.minimum(tallies[donor] - 1, limit - tallies[taker]) // 2
    room = jnp.where((donor == order[0]) | (taker == order[0]) | (tallies[taker] == 0), 0, jnp.maximum(room, 0))
    passed = jax.random.randint(jax.random.fold_in(own, 4), (amount // 2,), 0, 1 << 20) % (room + 1)
    tallies = tallies.at[donor].add(-passed).at[taker].add(passed)
    items = jnp.searchsorted(jnp.cumsum(tallies), jnp.arange(rows * top), side="right").astype(jnp.int32)
    grid = items.reshape(top, rows).T
    grid = grid[jax.random.permutation(jax.random.fold_in(own, 1), rows)]
    turn = jax.random.randint(jax.random.fold_in(own, 2), (rows, 1), 0, top)
    return jnp.take_along_axis(grid, (jnp.arange(top)[None, :] + turn) % top, axis=1)


def portions_of(count, total, reach, skew, full):
    portions = [(1 << 20) // math.isqrt(standing ** skew) + 1 for standing in range(1, count + 1)]
    largest = reach if full else min(reach, max(-(-total // count), total * portions[0] // sum(portions)))
    least = 1 if total - largest >= count - 1 else 0
    counts, spare = [largest] + [least] * (count - 1), total - largest - least * (count - 1)
    while spare > 0:
        candidates = [i for i in range(1, count) if counts[i] < largest] or [i for i in range(1, count) if counts[i] < reach]
        pool, left = sum([portions[i] for i in candidates]), spare
        for i in candidates:
            extra = min(reach - counts[i], max(1, left * portions[i] // pool), spare)
            counts[i] = counts[i] + extra
            spare = spare - extra
    return np.array(counts)


def centred(stream_key, dims, deviation, reach, shards=(), kind=jnp.bfloat16):
    gain = levels(stream_key, dims, shards, -0.22, 0.18) if shards else 1.0
    array = jax.random.normal(stream_key, dims, jnp.float32) * deviation * gain
    return jnp.minimum(jnp.maximum(array, -reach), reach).astype(kind)


def setup_inputs(seed: int = 0) -> dict:
    key_of = jax.random.split(jax.random.key(seed), 12)
    sky_model = centred(key_of[0], (NSTRIP, NSEG, BLOCK_ROWS), 1.0, 6.0, ((0, 4), (1, 8)))
    observed = centred(key_of[1], (NSTRIP, NRB, COLS, BLOCK_ROWS), 1.0, 6.0, ((0, 4), (1, 8)))
    row_weight = jnp.clip(jnp.exp(math.log(1.0) - 2.3025851 * jax.random.uniform(key_of[2], (NSTRIP, NRB, BLOCK_ROWS), jnp.float32) ** levels(key_of[2], (NSTRIP, NRB, BLOCK_ROWS), ((0, 4), (1, 8)), -0.2, 0.2)), 0.1, 1.0)
    foot_owner_keys = jax.random.split(jax.random.fold_in(key_of[3], 1), NSTRIP * NRB * COLS // (RB_DEV * COLS))
    foot_owner_turns = jax.random.permutation(jax.random.fold_in(key_of[3], 3), NSTRIP * NRB * COLS // (RB_DEV * COLS))
    foot_owner = jax.vmap(lambda own, number: assign_block(jax.random.fold_in(key_of[3], 2), own, number, RB_DEV * COLS, N_TILE, 1, CAP, 2))(foot_owner_keys, foot_owner_turns).reshape((NSTRIP, NRB, COLS, 1))
    foot_local = plant(jax.random.randint(key_of[4], (NSTRIP, NRB, COLS), 0, SEG_DEV), jax.random.fold_in(key_of[4], 1), 0, SEG_DEV - 1).astype(jnp.int32)
    row_offset = plant(jax.random.randint(key_of[5], (NSTRIP, NRB), -4, 5), jax.random.fold_in(key_of[5], 1), -4, 4).astype(jnp.int32)
    exposure_of = plant(jax.random.randint(key_of[6], (NSTRIP, NRB), 0, EXPO), jax.random.fold_in(key_of[6], 1), 0, EXPO - 1).astype(jnp.int32)
    amplitude = jnp.clip(jnp.exp(jax.random.uniform(key_of[7], (COMPS, EXPO), jnp.float32, math.log(0.25), math.log(1.0))), 0.25, 1.0)
    subpixel_shift = jnp.clip(jax.random.uniform(key_of[8], (EXPO,), jnp.float32, 0.05, 0.95), 0.05, 0.95)
    column_profile = jnp.clip(jax.random.uniform(key_of[9], (EXPO, COMPS, TAPS), jnp.float32, 0.05, 0.3), 0.05, 0.3)
    row_profile = jnp.clip(jax.random.uniform(key_of[10], (EXPO, COMPS, TAPS), jnp.float32, 0.05, 0.3), 0.05, 0.3)
    return dict(sky_model=sky_model, observed=observed, row_weight=row_weight, foot_owner=foot_owner, foot_local=foot_local, row_offset=row_offset, exposure_of=exposure_of, amplitude=amplitude, subpixel_shift=subpixel_shift, column_profile=column_profile, row_profile=row_profile)


def band_matrix(profile, size):
    taps = profile.shape[-1]
    out_index = jnp.arange(size, dtype=jnp.int32)[:, None]
    in_index = jnp.arange(size, dtype=jnp.int32)[None, :]
    lag = in_index - out_index + taps // 2
    inside = (lag >= 0) & (lag < taps)
    picked = profile[..., jnp.clip(lag, 0, taps - 1)]
    return jnp.where(inside, picked, jnp.zeros_like(picked))


def one_block(inputs):
    fetched, observed_block, weight_rows, offset, frac, amps, wide_profile, tall_profile = inputs
    width = fetched.shape[0]
    rows = fetched.shape[1]
    pixels = width * rows
    j_index = jnp.arange(rows, dtype=jnp.int32)[:, None]
    v_index = jnp.arange(rows, dtype=jnp.int32)[None, :]
    lower_hit = j_index == v_index + offset
    upper_hit = j_index == v_index + offset + 1
    zero_b = jnp.zeros((), jnp.bfloat16)
    weight_low = (1.0 - frac).astype(jnp.bfloat16)
    weight_high = frac.astype(jnp.bfloat16)
    interp = jnp.where(lower_hit, weight_low, zero_b) + jnp.where(upper_hit, weight_high, zero_b)
    slope_map = upper_hit.astype(jnp.float32) - lower_hit.astype(jnp.float32)
    resampled = jnp.dot(fetched, interp, preferred_element_type=jnp.float32).astype(jnp.bfloat16)
    tall = band_matrix(lax.optimization_barrier(tall_profile.astype(jnp.bfloat16)), rows).astype(jnp.float32)
    wide = band_matrix(lax.optimization_barrier(wide_profile.astype(jnp.bfloat16)), width).astype(jnp.float32)
    blurred = jnp.einsum('uw,qvw->quv', resampled.astype(jnp.float32), tall).astype(jnp.bfloat16)
    component = jnp.einsum('qux,qxv->quv', wide, blurred.astype(jnp.float32))
    model = jnp.sum(amps[:, None, None] * component, axis=0)
    weighted = weight_rows[None, :] * (model - observed_block.astype(jnp.float32))
    amp_term = jnp.sum(component * weighted[None], axis=(1, 2)) / pixels
    residual_b = weighted.astype(jnp.bfloat16)
    back_wide = jnp.einsum('qxu,xv->quv', wide, residual_b.astype(jnp.float32)).astype(jnp.bfloat16)
    image_adjoint = jnp.sum(amps[:, None, None] * jnp.einsum('quv,qvw->quw', back_wide.astype(jnp.float32), tall), axis=0)
    adjoint_b = image_adjoint.astype(jnp.bfloat16)
    slope = jnp.dot(fetched.astype(jnp.float32), slope_map, precision=lax.Precision.HIGHEST)
    shift_term = jnp.sum(image_adjoint * slope) / pixels
    segment_grad = jnp.dot(adjoint_b, interp.T, preferred_element_type=jnp.float32)
    return segment_grad, amp_term, shift_term


def reference(sky_model, observed, row_weight, foot_owner, foot_local, row_offset, exposure_of, amplitude, subpixel_shift, column_profile, row_profile):
    strips = sky_model.shape[0]
    seg_total = sky_model.shape[1]
    rows = sky_model.shape[2]
    block_total = observed.shape[1]
    width = observed.shape[2]
    seg_index = foot_owner[..., 0] * SEG_DEV + foot_local
    strip_base = (jnp.arange(strips, dtype=jnp.int32) * seg_total)[:, None, None]
    global_index = (seg_index + strip_base).astype(jnp.int32).reshape(strips * block_total, width)
    flat_sky = sky_model.reshape(strips * seg_total, rows)
    expo_flat = exposure_of.reshape(strips * block_total).astype(jnp.int32)

    def per_block(items):
        index_row, observed_block, weight_rows, offset, expo = items
        fetched = jnp.take(flat_sky, index_row, axis=0)
        return one_block((fetched, observed_block, weight_rows, offset, subpixel_shift[expo], amplitude[:, expo], column_profile[expo], row_profile[expo]))

    segment_grad, amp_term, shift_term = lax.map(per_block, (global_index, observed.reshape(strips * block_total, width, rows), row_weight.reshape(strips * block_total, rows), row_offset.reshape(strips * block_total).astype(jnp.int32), expo_flat))
    grad_flat = jnp.zeros((strips * seg_total, rows), jnp.float32).at[global_index.reshape(-1)].add(segment_grad.reshape(-1, rows))
    grad_sky = grad_flat.reshape(strips, seg_total, rows)
    amp_sums = jax.ops.segment_sum(amp_term, expo_flat, num_segments=EXPO)
    shift_sums = jax.ops.segment_sum(shift_term, expo_flat, num_segments=EXPO)
    grad_params = jnp.concatenate([amp_sums.T, shift_sums[None, :]], axis=0)
    return grad_sky, grad_params
```

```python
import functools

import jax
import jax.numpy as jnp
from jax import lax
from jax.experimental import pallas as pl
from jax.experimental.pallas import tpu as pltpu
from jax.sharding import PartitionSpec as P

MESH = pl.DeviceIdType.MESH
BF = jnp.bfloat16
F32 = jnp.float32
TN = (((0,), (0,)), ((), ()))
NT = (((1,), (1,)), ((), ()))


def iota(shape, dim):
    return lax.broadcasted_iota(jnp.int32, shape, dim)


def dot(a, b):
    return jnp.dot(a, b, preferred_element_type=F32)


def onehot(hit):
    return jnp.where(hit, 1.0, 0.0).astype(BF)


def bands(taps_b, rev):
    comps, taps = taps_b.shape
    place_t = iota((taps, 256), 0)
    place_m = iota((taps, 256), 1) - (128 - taps // 2)
    place = onehot(place_m == ((taps - 1 - place_t) if rev else place_t))
    base = dot(taps_b, place)
    x = jnp.concatenate(
        [jnp.broadcast_to(base[q : q + 1], (128, 256)) for q in range(comps)], axis=0
    )
    row = iota(x.shape, 0)
    for bit in range(7):
        x = jnp.where((row & (1 << bit)) != 0, pltpu.roll(x, 1 << bit, 1), x)
    return x


def kernel(
    tiles,
    nband,
    cap,
    owner_ref,
    local_ref,
    weight_ref,
    offset_ref,
    expo_ref,
    amp_ref,
    frac_ref,
    sky_hbm,
    obs_hbm,
    col_hbm,
    rowp_hbm,
    grad_ref,
    params_ref,
    sky,
    obs,
    colp,
    rowp,
    hits,
    picks,
    req_out,
    req_in,
    rows_out,
    rows_in,
    grads_out,
    grads_in,
    terms_out,
    terms_in,
    part_out,
    part_in,
    fet,
    blur,
    fwd,
    bwd,
    tall,
    tall_t,
    obs_t,
    resid,
    comp,
    back,
    seg_grad,
    total,
    load_sem,
    req_s,
    req_r,
    rows_s,
    rows_r,
    grads_s,
    grads_r,
    terms_s,
    terms_r,
    part_s,
    part_r,
):
    me = lax.axis_index("tile")
    band = lax.axis_index("band")
    segs, rows = sky.shape
    width = obs.shape[0]
    comps = blur.shape[0]
    pixels = width * rows
    nblk = width // 256

    loads = [
        pltpu.make_async_copy(src, dst, load_sem.at[i])
        for i, (src, dst) in enumerate(
            ((sky_hbm, sky), (obs_hbm, obs), (col_hbm, colp), (rowp_hbm, rowp))
        )
    ]
    for load in loads:
        load.start()

    barrier = pltpu.get_barrier_semaphore()

    def greet_tile(k, c):
        pl.semaphore_signal(
            barrier, inc=1, device_id={"tile": lax.rem(me + 1 + k, tiles)}, device_id_type=MESH
        )
        return c

    def greet_band(k, c):
        pl.semaphore_signal(
            barrier, inc=1, device_id={"band": lax.rem(band + 1 + k, nband)}, device_id_type=MESH
        )
        return c

    lax.fori_loop(0, tiles - 1, greet_tile, 0)
    lax.fori_loop(0, nband - 1, greet_band, 0)

    def after(k):
        return lax.rem(me + 1 + k, tiles)

    def ahead(k):
        return lax.rem(me + (tiles - 1) - k, tiles)

    def push(src, dst, send, recv, p):
        return pltpu.make_async_remote_copy(
            src_ref=src.at[p],
            dst_ref=dst.at[me],
            send_sem=send.at[p],
            recv_sem=recv.at[me],
            device_id={"tile": p},
            device_id_type=MESH,
        )

    def arrival(src, dst, send, recv, p):
        return pltpu.make_async_remote_copy(
            src_ref=src.at[p],
            dst_ref=dst.at[p],
            send_sem=send.at[p],
            recv_sem=recv.at[p],
            device_id={"tile": p},
            device_id_type=MESH,
        )

    owner = owner_ref[...]
    member = jnp.where(iota((tiles, width), 0) == owner, 1.0, 0.0)
    pieces = [member[:, b * 128 : (b + 1) * 128] for b in range(width // 128)]
    above = onehot(iota((128, 128), 0) < iota((128, 128), 1))
    prefix = dot(jnp.concatenate(pieces, axis=0).astype(BF), above)
    run = jnp.zeros((tiles, 1), F32)
    ranks = []
    for b, piece in enumerate(pieces):
        earlier = prefix[b * tiles : (b + 1) * tiles] + run
        ranks.append(jnp.sum(piece * earlier, axis=0, keepdims=True))
        run = run + jnp.sum(piece, axis=1, keepdims=True)
    slot = owner * cap + jnp.concatenate(ranks, axis=1).astype(jnp.int32)
    wanted = local_ref[...] + 1
    which = iota((16, width), 0)
    digits = (
        jnp.where(which == 0, wanted >> 6, jnp.where(which == 1, wanted & 63, 0))
        .astype(F32)
        .astype(BF)
    )

    pl.semaphore_wait(barrier, tiles - 1 + nband - 1)

    def ask(p, out):
        hit = onehot(iota((cap, width), 0) + p * cap == slot)
        hits[p] = hit
        ids = lax.dot_general(digits, hit, NT, preferred_element_type=F32)
        out[p] = ids[0:1] * 64.0 + ids[1:2]

    def ask_peer(k, c):
        p = after(k)
        ask(p, req_out)
        push(req_out, req_in, req_s, req_r, p).start()
        return c

    lax.fori_loop(0, tiles - 1, ask_peer, 0)
    ask(me, req_in)
    loads[0].wait()

    def serve(p):
        ids = jnp.broadcast_to(req_in[p], (128, cap)).T
        lane = iota((cap, 128), 1).astype(F32)
        for b in range(segs // 128):
            picks[p, :, b * 128 : (b + 1) * 128] = onehot(ids == lane + float(b * 128 + 1))
        rows_out[p] = dot(picks[p], sky[...]).astype(BF)

    def serve_peer(k, c):
        p = ahead(k)
        arrival(req_out, req_in, req_s, req_r, p).wait_recv()
        serve(p)
        push(rows_out, rows_in, rows_s, rows_r, p).start()
        return c

    lax.fori_loop(0, tiles - 1, serve_peer, 0)
    serve(me)

    for load in loads[1:]:
        load.wait()
    expo = expo_ref[0, 0]
    offset = offset_ref[0, 0]
    amps = [amp_ref[q, expo] for q in range(comps)]
    col_b = colp[expo].astype(BF)
    row_b = rowp[expo].astype(BF)
    low = iota((128, 128), 1) < 64
    for rev, wide in ((True, fwd), (False, bwd)):
        made = bands(col_b, rev)
        zero = jnp.zeros((128, 128), F32)
        for q in range(comps):
            edge = made[q * 128 : (q + 1) * 128, :128]
            mid = made[q * 128 : (q + 1) * 128, 128:].astype(BF)
            left = jnp.where(low, 0.0, edge).astype(BF)
            right = jnp.where(low, edge, 0.0).astype(BF)
            none = zero.astype(BF)
            line = [none, left, mid, right, none, none]
            for b in range(4):
                for h in range(2):
                    at = h + 3 - b
                    at = at if 0 <= at < 6 else 0
                    wide[q, b * 128 : (b + 1) * 128, h * 128 : (h + 1) * 128] = line[at]
    made = bands(row_b, False)
    for q in range(comps):
        tall[q * 128 : (q + 1) * 128, :] = made[q * 128 : (q + 1) * 128, 128:].astype(BF)
    made = bands(row_b, True)
    for q in range(comps):
        tall_t[:, q * 128 : (q + 1) * 128] = made[q * 128 : (q + 1) * 128, 128:].astype(BF)
    for b in range(width // 128):
        i, h = b // 2, b % 2
        obs_t[i * 128 : (i + 1) * 128, h * 128 : (h + 1) * 128] = (
            obs[b * 128 : (b + 1) * 128, :].astype(F32).T
        )
    heavy = jnp.broadcast_to(weight_ref[...], (128, 128)).T
    frac = jnp.full((128, 128), frac_ref[expo], F32)
    w_low = (1.0 - frac).astype(BF).astype(F32)
    w_high = frac.astype(BF).astype(F32)
    sub, lane = iota((128, 128), 0), iota((128, 128), 1)
    interp_t = (
        jnp.where(lane == sub + offset, w_low, 0.0)
        + jnp.where(lane == sub + offset + 1, w_high, 0.0)
    ).astype(BF)
    interp = (
        jnp.where(sub == lane + offset, w_low, 0.0)
        + jnp.where(sub == lane + offset + 1, w_high, 0.0)
    ).astype(BF)
    slope_t = (
        jnp.where(lane == sub + offset + 1, 1.0, 0.0) - jnp.where(lane == sub + offset, 1.0, 0.0)
    ).astype(BF)
    blank = jnp.zeros((128, 128), BF)
    for q in range(comps):
        blur[q, :, :128] = blank
        blur[q, :, 128 + width :] = blank
    resid[:, :128] = blank
    resid[:, 128 + width :] = blank

    fet[...] = lax.dot_general(rows_out[me], hits[me], TN, preferred_element_type=F32)

    def take(k, c):
        p = after(k)
        arrival(rows_out, rows_in, rows_s, rows_r, p).wait_recv()
        fet[...] += lax.dot_general(rows_in[p], hits[p], TN, preferred_element_type=F32)
        return c

    lax.fori_loop(0, tiles - 1, take, 0)

    fetched = fet[...].astype(BF)
    resampled = dot(interp_t, fetched).astype(BF)
    for q in range(comps):
        blur[q, :, 128 : 128 + width] = dot(tall[q * 128 : (q + 1) * 128, :], resampled).astype(BF)
    model = None
    for q in range(comps):
        left = jnp.concatenate([blur[q, :, i * 256 : i * 256 + 512] for i in range(nblk)], axis=0)
        part = dot(left, fwd[q])
        comp[q] = part
        model = amps[q] * part if model is None else model + amps[q] * part
    scale = jnp.concatenate([jnp.concatenate([heavy, heavy], axis=1)] * nblk, axis=0)
    weighted = scale * (model - obs_t[...])
    terms = [
        jnp.sum(jnp.sum(comp[q] * weighted, axis=0, keepdims=True), axis=1, keepdims=True) / pixels
        for q in range(comps)
    ]
    weighted_b = weighted.astype(BF)
    for i in range(nblk):
        resid[:, 128 + i * 256 : 128 + (i + 1) * 256] = weighted_b[i * 128 : (i + 1) * 128]
    left = jnp.concatenate([resid[:, i * 256 : i * 256 + 512] for i in range(nblk)], axis=0)
    for q in range(comps):
        back[q] = (amps[q] * dot(left, bwd[q])).astype(BF)
    shift = jnp.zeros((128, 256), F32)
    for i in range(nblk):
        stack = jnp.concatenate(
            [back[q, i * 128 : (i + 1) * 128, :] for q in range(comps)], axis=0
        )
        adjoint = dot(tall_t[...], stack)
        shift = shift + adjoint * dot(slope_t, fetched[:, i * 256 : (i + 1) * 256])
        seg_grad[i * 256 : (i + 1) * 256, :] = dot(interp, adjoint.astype(BF)).T.astype(BF)
    terms.append(jnp.sum(jnp.sum(shift, axis=0, keepdims=True), axis=1, keepdims=True) / pixels)

    line = iota((8, 128), 0)
    card = jnp.where(line == 5, expo.astype(F32), 0.0)
    for q, term in enumerate(terms):
        card = jnp.where(line == q, jnp.broadcast_to(term, (8, 128)), card)
    terms_out[...] = card
    terms_in[me] = card

    def tell(p):
        return pltpu.make_async_remote_copy(
            src_ref=terms_out,
            dst_ref=terms_in.at[me],
            send_sem=terms_s.at[p],
            recv_sem=terms_r.at[me],
            device_id={"tile": p},
            device_id_type=MESH,
        )

    def tell_peer(k, c):
        tell(after(k)).start()
        return c

    lax.fori_loop(0, tiles - 1, tell_peer, 0)

    def give(p):
        grads_out[p] = dot(hits[p], seg_grad[...]).astype(BF)

    def give_peer(k, c):
        p = after(k)
        give(p)
        push(grads_out, grads_in, grads_s, grads_r, p).start()
        return c

    lax.fori_loop(0, tiles - 1, give_peer, 0)
    give(me)

    def hear(k, c):
        p = ahead(k)
        pltpu.make_async_remote_copy(
            src_ref=terms_out,
            dst_ref=terms_in.at[p],
            send_sem=terms_s.at[p],
            recv_sem=terms_r.at[p],
            device_id={"tile": p},
            device_id_type=MESH,
        ).wait_recv()
        return c

    lax.fori_loop(0, tiles - 1, hear, 0)
    expos = params_ref.shape[1]
    column = iota((8, 128), 1).astype(F32)

    def gather_terms(t, acc):
        block = terms_in[t]
        named = block[5:6, :]
        return tuple(
            a + jnp.where(column + float(128 * b) == named, block, 0.0) for b, a in enumerate(acc)
        )

    acc = lax.fori_loop(
        0,
        tiles,
        gather_terms,
        tuple(jnp.zeros((8, 128), F32) for _ in range(expos // 128)),
    )
    whole = jnp.concatenate(acc, axis=1)
    part_out[...] = whole
    part_in[band] = whole

    def share(k, here):
        to = lax.rem(band + 1 + k, nband)
        return pltpu.make_async_remote_copy(
            src_ref=part_out,
            dst_ref=part_in.at[band] if here else part_in.at[to],
            send_sem=part_s.at[to],
            recv_sem=part_r.at[band] if here else part_r.at[to],
            device_id={"band": to},
            device_id_type=MESH,
        )

    for k in range(nband - 1):
        share(k, True).start()

    total[...] = lax.dot_general(grads_out[me], picks[me], TN, preferred_element_type=F32)

    def collect(k, c):
        p = ahead(k)
        arrival(grads_out, grads_in, grads_s, grads_r, p).wait_recv()
        total[...] += lax.dot_general(grads_in[p], picks[p], TN, preferred_element_type=F32)
        return c

    lax.fori_loop(0, tiles - 1, collect, 0)
    for b in range(segs // 128):
        grad_ref[b * 128 : (b + 1) * 128, :] = total[:, b * 128 : (b + 1) * 128].T

    for k in range(nband - 1):
        share(k, False).wait_recv()
    summed = part_in[0]
    for b in range(1, nband):
        summed = summed + part_in[b]
    params_ref[...] = summed[: comps + 1]

    def settle(k, c):
        p = after(k)
        push(req_out, req_in, req_s, req_r, p).wait_send()
        push(rows_out, rows_in, rows_s, rows_r, p).wait_send()
        push(grads_out, grads_in, grads_s, grads_r, p).wait_send()
        tell(p).wait_send()
        return c

    lax.fori_loop(0, tiles - 1, settle, 0)
    for k in range(nband - 1):
        share(k, True).wait_send()


def body(
    sky_model,
    observed,
    row_weight,
    foot_owner,
    foot_local,
    row_offset,
    exposure_of,
    amplitude,
    subpixel_shift,
    column_profile,
    row_profile,
):
    tiles = lax.axis_size("tile")
    nband = lax.axis_size("band")
    segs, rows = sky_model.shape[1:]
    width = observed.shape[2]
    comps, expos = amplitude.shape
    taps = column_profile.shape[2]
    cap = 2 * width // tiles
    vmem = pl.BlockSpec(memory_space=pltpu.VMEM)
    smem = pl.BlockSpec(memory_space=pltpu.SMEM)
    hbm = pl.BlockSpec(memory_space=pl.ANY)
    dma = pltpu.SemaphoreType.DMA
    grad, params = pl.pallas_call(
        functools.partial(kernel, tiles, nband, cap),
        out_shape=(
            jax.ShapeDtypeStruct((segs, rows), F32),
            jax.ShapeDtypeStruct((comps + 1, expos), F32),
        ),
        in_specs=[vmem, vmem, vmem, smem, smem, smem, smem, hbm, hbm, hbm, hbm],
        out_specs=(vmem, vmem),
        scratch_shapes=[
            pltpu.VMEM((segs, rows), BF),
            pltpu.VMEM((width, rows), BF),
            pltpu.VMEM((expos, comps, taps), F32),
            pltpu.VMEM((expos, comps, taps), F32),
            pltpu.VMEM((tiles, cap, width), BF),
            pltpu.VMEM((tiles, cap, segs), BF),
            pltpu.VMEM((tiles, 1, cap), F32),
            pltpu.VMEM((tiles, 1, cap), F32),
            pltpu.VMEM((tiles, cap, rows), BF),
            pltpu.VMEM((tiles, cap, rows), BF),
            pltpu.VMEM((tiles, cap, rows), BF),
            pltpu.VMEM((tiles, cap, rows), BF),
            pltpu.VMEM((8, 128), F32),
            pltpu.VMEM((tiles, 8, 128), F32),
            pltpu.VMEM((8, expos), F32),
            pltpu.VMEM((nband, 8, expos), F32),
            pltpu.VMEM((rows, width), F32),
            pltpu.VMEM((comps, rows, width + 256), BF),
            pltpu.VMEM((comps, 512, 256), BF),
            pltpu.VMEM((comps, 512, 256), BF),
            pltpu.VMEM((comps * rows, rows), BF),
            pltpu.VMEM((rows, comps * rows), BF),
            pltpu.VMEM((width // 256 * rows, 256), F32),
            pltpu.VMEM((rows, width + 256), BF),
            pltpu.VMEM((comps, width // 256 * rows, 256), F32),
            pltpu.VMEM((comps, width // 256 * rows, 256), BF),
            pltpu.VMEM((width, rows), BF),
            pltpu.VMEM((rows, segs), F32),
            dma((4,)),
        ]
        + [dma((tiles,))] * 8
        + [dma((nband,))] * 2,
        compiler_params=pltpu.CompilerParams(
            collective_id=0, has_side_effects=True, vmem_limit_bytes=52 * 1024 * 1024
        ),
    )(
        foot_owner.reshape(1, width),
        foot_local.reshape(1, width),
        row_weight.reshape(1, rows),
        row_offset,
        exposure_of,
        amplitude,
        subpixel_shift,
        sky_model[0],
        observed[0, 0],
        column_profile,
        row_profile,
    )
    return (grad[None], params)


def solution(mesh):
    placed = (
        P("band", "tile", None),
        P("band", "tile", None, None),
        P("band", "tile", None),
        P("band", "tile", None, None),
        P("band", "tile", None),
        P("band", "tile"),
        P("band", "tile"),
        P(),
        P(),
        P(),
        P(),
    )
    return jax.shard_map(
        body, mesh=mesh, in_specs=placed, out_specs=(P("band", "tile", None), P()), check_vma=False
    )
```

```python
import functools

import jax
import jax.numpy as jnp
from jax import lax
from jax.experimental import pallas as pl
from jax.experimental.pallas import tpu as pltpu
from jax.sharding import PartitionSpec as P

MESH = pl.DeviceIdType.MESH
BF = jnp.bfloat16
F32 = jnp.float32
TN = (((0,), (0,)), ((), ()))
NT = (((1,), (1,)), ((), ()))


def iota(shape, dim):
    return lax.broadcasted_iota(jnp.int32, shape, dim)


def dot(a, b):
    return jnp.dot(a, b, preferred_element_type=F32)


def onehot(hit):
    return jnp.where(hit, 1.0, 0.0).astype(BF)


def spread(ref, expo):
    taps, comps, expos = ref.shape
    named = iota((comps, expos), 1) == expo
    lane = iota((comps, 256), 1) - (128 - taps // 2)
    straight = mirrored = jnp.zeros((comps, 256), F32)
    for t in range(taps):
        tap = jnp.sum(jnp.where(named, ref[t], 0.0), axis=1, keepdims=True)
        straight = jnp.where(lane == t, tap, straight)
        mirrored = jnp.where(lane == taps - 1 - t, tap, mirrored)
    return straight.astype(BF).astype(F32), mirrored.astype(BF).astype(F32)


def bands(base):
    comps = base.shape[0]
    x = jnp.concatenate(
        [jnp.broadcast_to(base[q : q + 1], (128, 256)) for q in range(comps)], axis=0
    )
    row = iota(x.shape, 0)
    for bit in range(7):
        x = jnp.where((row & (1 << bit)) != 0, pltpu.roll(x, 1 << bit, 1), x)
    return x


def steps(low, high, work):
    if high - low <= 8:
        for k in range(low, high):
            work(k)
    else:
        lax.fori_loop(low, high, lambda k, c: (work(k), c)[1], 0)


def kernel(
    tiles,
    nband,
    cap,
    owner_ref,
    local_ref,
    weight_ref,
    offset_ref,
    expo_ref,
    amp_ref,
    frac_ref,
    sky_hbm,
    obs_hbm,
    col_hbm,
    rowp_hbm,
    total,
    summed_ref,
    sky,
    obs,
    colp,
    rowp,
    hits,
    picks,
    req_out,
    req_in,
    rows_out,
    rows_in,
    grads_out,
    grads_in,
    card_out,
    cards,
    part_out,
    part_in,
    fet,
    blur,
    fwd,
    bwd,
    tall,
    tall_t,
    obs_t,
    resid,
    back_f,
    back,
    adj,
    seg_grad,
    load_sem,
    req_s,
    req_r,
    rows_s,
    rows_r,
    grads_s,
    grads_r,
    cards_s,
    cards_r,
    part_s,
    part_r,
):
    me = lax.axis_index("tile")
    band = lax.axis_index("band")
    segs, rows = sky.shape
    width = obs.shape[0]
    comps = blur.shape[0]
    pixels = width * rows
    nblk = width // 256

    loads = [
        pltpu.make_async_copy(src, dst, load_sem.at[i])
        for i, (src, dst) in enumerate(
            ((sky_hbm, sky), (obs_hbm, obs), (col_hbm, colp), (rowp_hbm, rowp))
        )
    ]
    for load in loads:
        load.start()

    barrier = pltpu.get_barrier_semaphore()

    def greet_tile(k, c):
        pl.semaphore_signal(
            barrier, inc=1, device_id={"tile": lax.rem(me + 1 + k, tiles)}, device_id_type=MESH
        )
        return c

    def greet_band(k, c):
        pl.semaphore_signal(
            barrier, inc=1, device_id={"band": lax.rem(band + 1 + k, nband)}, device_id_type=MESH
        )
        return c

    lax.fori_loop(0, tiles - 1, greet_tile, 0)
    lax.fori_loop(0, nband - 1, greet_band, 0)

    def peer(k):
        bits = [1 << b for b in range(tiles.bit_length() - 1)]
        return sum(lax.rem(me // bit + k // bit, 2) * bit for bit in bits)

    def push(src, dst, send, recv, p):
        return pltpu.make_async_remote_copy(
            src_ref=src.at[p],
            dst_ref=dst.at[me],
            send_sem=send.at[p],
            recv_sem=recv.at[me],
            device_id={"tile": p},
            device_id_type=MESH,
        )

    def arrival(src, dst, send, recv, p):
        return pltpu.make_async_remote_copy(
            src_ref=src.at[p],
            dst_ref=dst.at[p],
            send_sem=send.at[p],
            recv_sem=recv.at[p],
            device_id={"tile": p},
            device_id_type=MESH,
        )

    owner = owner_ref[...]
    member = jnp.where(iota((tiles, width), 0) == owner, 1.0, 0.0)
    pieces = [member[:, b * 128 : (b + 1) * 128] for b in range(width // 128)]
    above = onehot(iota((128, 128), 0) < iota((128, 128), 1))
    prefix = dot(jnp.concatenate(pieces, axis=0).astype(BF), above)
    run = jnp.zeros((tiles, 1), F32)
    ranks = []
    for b, piece in enumerate(pieces):
        earlier = prefix[b * tiles : (b + 1) * tiles] + run
        ranks.append(jnp.sum(piece * earlier, axis=0, keepdims=True))
        run = run + jnp.sum(piece, axis=1, keepdims=True)
    slot = owner * cap + jnp.concatenate(ranks, axis=1).astype(jnp.int32)
    wanted = local_ref[...] + 1
    which = iota((16, width), 0)
    digits = (
        jnp.where(which == 0, wanted >> 6, jnp.where(which == 1, wanted & 63, 0))
        .astype(F32)
        .astype(BF)
    )

    pl.semaphore_wait(barrier, tiles - 1 + nband - 1)

    def ask(p, out):
        hit = onehot(iota((cap, width), 0) + p * cap == slot)
        hits[p] = hit
        ids = lax.dot_general(digits, hit, NT, preferred_element_type=F32)
        out[p] = ids[0:1] * 64.0 + ids[1:2]

    def ask_peer(k):
        p = peer(k)
        ask(p, req_out)
        push(req_out, req_in, req_s, req_r, p).start()

    half = tiles // 2
    steps(half, tiles, ask_peer)
    loads[0].wait()

    def serve(p):
        ids = jnp.broadcast_to(req_in[p], (128, cap)).T
        lane = iota((cap, 128), 1).astype(F32)
        for b in range(segs // 128):
            picks[p, :, b * 128 : (b + 1) * 128] = onehot(ids == lane + float(b * 128 + 1))
        rows_out[p] = dot(picks[p], sky[...]).astype(BF)

    def serve_peer(k):
        p = peer(k)
        arrival(req_out, req_in, req_s, req_r, p).wait_recv()
        serve(p)
        push(rows_out, rows_in, rows_s, rows_r, p).start()

    def both(k):
        ask_peer(k)
        serve_peer(half + k - 1)

    steps(1, half, both)
    serve_peer(tiles - 1)
    steps(1, half, serve_peer)
    ask(me, req_in)
    serve(me)

    for load in loads[1:]:
        load.wait()
    expo = expo_ref[0, 0]
    offset = offset_ref[0, 0]
    amps = [amp_ref[q, expo] for q in range(comps)]
    col, col_mirror = spread(colp, expo)
    row, row_mirror = spread(rowp, expo)
    low = iota((128, 128), 1) < 64
    for base, wide in ((col_mirror, fwd), (col, bwd)):
        made = bands(base)
        zero = jnp.zeros((128, 128), F32)
        for q in range(comps):
            edge = made[q * 128 : (q + 1) * 128, :128]
            mid = made[q * 128 : (q + 1) * 128, 128:].astype(BF)
            left = jnp.where(low, 0.0, edge).astype(BF)
            right = jnp.where(low, edge, 0.0).astype(BF)
            none = zero.astype(BF)
            line = [none, left, mid, right, none, none]
            for b in range(4):
                for h in range(2):
                    at = h + 3 - b
                    at = at if 0 <= at < 6 else 0
                    wide[q, b * 128 : (b + 1) * 128, h * 128 : (h + 1) * 128] = line[at]
    made = bands(row)
    for q in range(comps):
        tall[q * 128 : (q + 1) * 128, :] = made[q * 128 : (q + 1) * 128, 128:].astype(BF)
    made = bands(row_mirror)
    for q in range(comps):
        tall_t[:, q * 128 : (q + 1) * 128] = made[q * 128 : (q + 1) * 128, 128:].astype(BF)
    for b in range(width // 128):
        i, h = b // 2, b % 2
        obs_t[i * 128 : (i + 1) * 128, h * 128 : (h + 1) * 128] = (
            obs[b * 128 : (b + 1) * 128, :].astype(F32).T
        )
    heavy = jnp.broadcast_to(weight_ref[...], (128, 128)).T
    frac = jnp.full((128, 128), frac_ref[expo], F32)
    w_low = (1.0 - frac).astype(BF).astype(F32)
    w_high = frac.astype(BF).astype(F32)
    sub, lane = iota((128, 128), 0), iota((128, 128), 1)
    interp_t = (
        jnp.where(lane == sub + offset, w_low, 0.0)
        + jnp.where(lane == sub + offset + 1, w_high, 0.0)
    ).astype(BF)
    interp = (
        jnp.where(sub == lane + offset, w_low, 0.0)
        + jnp.where(sub == lane + offset + 1, w_high, 0.0)
    ).astype(BF)
    slope_t = (
        jnp.where(lane == sub + offset + 1, 1.0, 0.0) - jnp.where(lane == sub + offset, 1.0, 0.0)
    ).astype(BF)
    blank = jnp.zeros((128, 128), BF)
    for q in range(comps):
        blur[q, :, :128] = blank
        blur[q, :, 128 + width :] = blank
    resid[:, :128] = blank
    resid[:, 128 + width :] = blank

    fet[...] = lax.dot_general(rows_out[me], hits[me], TN, preferred_element_type=F32)

    def take(k):
        p = peer(k)
        arrival(rows_out, rows_in, rows_s, rows_r, p).wait_recv()
        fet[...] += lax.dot_general(rows_in[p], hits[p], TN, preferred_element_type=F32)

    steps(half, tiles - 2, take)
    steps(1, half, take)
    steps(tiles - 2, tiles, take)

    fetched = fet[...].astype(BF)
    resampled = dot(interp_t, fetched).astype(BF)
    for q in range(comps):
        blur[q, :, 128 : 128 + width] = (
            amps[q] * dot(tall[q * 128 : (q + 1) * 128, :], resampled)
        ).astype(BF)
    model = None
    for q in range(comps):
        left = jnp.concatenate([blur[q, :, i * 256 : i * 256 + 512] for i in range(nblk)], axis=0)
        part = dot(left, fwd[q])
        model = part if model is None else model + part
    scale = jnp.concatenate([jnp.concatenate([heavy, heavy], axis=1)] * nblk, axis=0)
    weighted_b = (scale * (model - obs_t[...])).astype(BF)
    for i in range(nblk):
        resid[:, 128 + i * 256 : 128 + (i + 1) * 256] = weighted_b[i * 128 : (i + 1) * 128]
    left = jnp.concatenate([resid[:, i * 256 : i * 256 + 512] for i in range(nblk)], axis=0)
    for q in range(comps):
        part = amps[q] * dot(left, bwd[q])
        back_f[q] = part
        back[q] = part.astype(BF)
    for i in range(nblk):
        stack = jnp.concatenate(
            [back[q, i * 128 : (i + 1) * 128, :] for q in range(comps)], axis=0
        )
        adjoint = dot(tall_t[...], stack)
        adj[:, i * 256 : (i + 1) * 256] = adjoint
        seg_grad[i * 256 : (i + 1) * 256, :] = dot(interp, adjoint.astype(BF)).T.astype(BF)

    def give(p):
        grads_out[p] = dot(hits[p], seg_grad[...]).astype(BF)

    def give_peer(k):
        p = peer(k)
        give(p)
        push(grads_out, grads_in, grads_s, grads_r, p).start()

    steps(half, tiles, give_peer)

    terms = []
    for q in range(comps):
        acc = jnp.zeros((128, 256), F32)
        for i in range(nblk):
            acc = acc + (
                blur[q, :, 128 + i * 256 : 128 + (i + 1) * 256].astype(F32)
                * back_f[q, i * 128 : (i + 1) * 128, :]
            )
        acc = jnp.sum(jnp.sum(acc, axis=0, keepdims=True), axis=1, keepdims=True)
        gain = jnp.full((1, 1), amps[q], F32)
        terms.append(acc / (gain * gain * pixels))
    shift = jnp.sum(adj[...] * dot(slope_t, fetched), axis=0, keepdims=True)
    terms.append(jnp.sum(shift, axis=1, keepdims=True) / pixels)

    line = iota((8, 128), 0)
    card = jnp.where(line == 5, expo.astype(F32), 0.0)
    for q, term in enumerate(terms):
        card = jnp.where(line == q, jnp.broadcast_to(term, (8, 128)), card)
    card_out[...] = card
    cards[band] = card

    def swap(src, dst, send, recv, k, here):
        to = lax.rem(band + 1 + k, nband)
        return pltpu.make_async_remote_copy(
            src_ref=src,
            dst_ref=dst.at[band] if here else dst.at[to],
            send_sem=send.at[to],
            recv_sem=recv.at[band] if here else recv.at[to],
            device_id={"band": to},
            device_id_type=MESH,
        )

    for k in range(nband - 1):
        swap(card_out, cards, cards_s, cards_r, k, True).start()

    steps(1, half, give_peer)
    give(me)

    for k in range(nband - 1):
        swap(card_out, cards, cards_s, cards_r, k, False).wait_recv()
    expos = summed_ref.shape[1]
    column = iota((8, expos), 1).astype(F32)
    part = jnp.zeros((8, expos), F32)
    for b in range(nband):
        block = jnp.concatenate([cards[b]] * (expos // 128), axis=1)
        part = part + jnp.where(column == block[5:6, :], block, 0.0)
    part_out[...] = part
    part_in[me] = part

    def tell(p, here):
        return pltpu.make_async_remote_copy(
            src_ref=part_out,
            dst_ref=part_in.at[me] if here else part_in.at[p],
            send_sem=part_s.at[p],
            recv_sem=part_r.at[me] if here else part_r.at[p],
            device_id={"tile": p},
            device_id_type=MESH,
        )

    steps(1, tiles, lambda k: tell(peer(k), True).start())

    total[...] = lax.dot_general(grads_out[me], picks[me], TN, preferred_element_type=F32)

    def collect(k):
        p = peer(k)
        arrival(grads_out, grads_in, grads_s, grads_r, p).wait_recv()
        total[...] += lax.dot_general(grads_in[p], picks[p], TN, preferred_element_type=F32)

    steps(half, tiles - 2, collect)
    steps(1, half, collect)
    steps(tiles - 2, tiles, collect)

    steps(1, tiles, lambda k: tell(peer(k), False).wait_recv())
    summed_ref[...] = lax.fori_loop(
        0, tiles, lambda t, acc: acc + part_in[t], jnp.zeros((8, expos), F32)
    )

    def settle(k):
        p = peer(k)
        push(req_out, req_in, req_s, req_r, p).wait_send()
        push(rows_out, rows_in, rows_s, rows_r, p).wait_send()
        push(grads_out, grads_in, grads_s, grads_r, p).wait_send()
        tell(p, True).wait_send()

    steps(1, tiles, settle)
    for k in range(nband - 1):
        swap(card_out, cards, cards_s, cards_r, k, True).wait_send()


def finish(total, summed, grad_ref, params_ref):
    rows = grad_ref.shape[0]
    at = pl.multiple_of(pl.program_id(0) * rows, rows)
    grad_ref[...] = total[:, pl.ds(at, rows)].T
    params_ref[...] = summed[: params_ref.shape[0]]


def body(
    sky_model,
    observed,
    row_weight,
    foot_owner,
    foot_local,
    row_offset,
    exposure_of,
    amplitude,
    subpixel_shift,
    column_profile,
    row_profile,
):
    tiles = lax.axis_size("tile")
    nband = lax.axis_size("band")
    segs, rows = sky_model.shape[1:]
    width = observed.shape[2]
    comps, expos = amplitude.shape
    taps = column_profile.shape[2]
    cap = 2 * width // tiles
    vmem = pl.BlockSpec(memory_space=pltpu.VMEM)
    smem = pl.BlockSpec(memory_space=pltpu.SMEM)
    hbm = pl.BlockSpec(memory_space=pltpu.HBM)
    dma = pltpu.SemaphoreType.DMA
    total, summed = pl.pallas_call(
        functools.partial(kernel, tiles, nband, cap),
        out_shape=(
            jax.ShapeDtypeStruct((rows, segs), F32),
            jax.ShapeDtypeStruct((8, expos), F32),
        ),
        in_specs=[vmem, vmem, vmem, smem, smem, smem, smem, hbm, hbm, hbm, hbm],
        out_specs=(vmem, vmem),
        scratch_shapes=[
            pltpu.VMEM((segs, rows), BF),
            pltpu.VMEM((width, rows), BF),
            pltpu.VMEM((taps, comps, expos), F32),
            pltpu.VMEM((taps, comps, expos), F32),
            pltpu.VMEM((tiles, cap, width), BF),
            pltpu.VMEM((tiles, cap, segs), BF),
            pltpu.VMEM((tiles, 1, cap), F32),
            pltpu.VMEM((tiles, 1, cap), F32),
            pltpu.VMEM((tiles, cap, rows), BF),
            pltpu.VMEM((tiles, cap, rows), BF),
            pltpu.VMEM((tiles, cap, rows), BF),
            pltpu.VMEM((tiles, cap, rows), BF),
            pltpu.VMEM((8, 128), F32),
            pltpu.VMEM((nband, 8, 128), F32),
            pltpu.VMEM((8, expos), F32),
            pltpu.VMEM((tiles, 8, expos), F32),
            pltpu.VMEM((rows, width), F32),
            pltpu.VMEM((comps, rows, width + 256), BF),
            pltpu.VMEM((comps, 512, 256), BF),
            pltpu.VMEM((comps, 512, 256), BF),
            pltpu.VMEM((comps * rows, rows), BF),
            pltpu.VMEM((rows, comps * rows), BF),
            pltpu.VMEM((width // 256 * rows, 256), F32),
            pltpu.VMEM((rows, width + 256), BF),
            pltpu.VMEM((comps, width // 256 * rows, 256), F32),
            pltpu.VMEM((comps, width // 256 * rows, 256), BF),
            pltpu.VMEM((rows, width), F32),
            pltpu.VMEM((width, rows), BF),
            dma((4,)),
        ]
        + [dma((tiles,))] * 6
        + [dma((nband,))] * 2
        + [dma((tiles,))] * 2,
        compiler_params=pltpu.CompilerParams(
            collective_id=0, has_side_effects=True, vmem_limit_bytes=36 * 1024 * 1024
        ),
    )(
        foot_owner.reshape(1, width),
        foot_local.reshape(1, width),
        row_weight.reshape(1, rows),
        row_offset,
        exposure_of,
        amplitude,
        subpixel_shift,
        sky_model[0],
        observed[0, 0],
        column_profile.transpose(2, 1, 0),
        row_profile.transpose(2, 1, 0),
    )
    piece = min(512, segs)
    grad, params = pl.pallas_call(
        finish,
        grid=(segs // piece,),
        out_shape=(
            jax.ShapeDtypeStruct((segs, rows), F32),
            jax.ShapeDtypeStruct((comps + 1, expos), F32),
        ),
        in_specs=[vmem, vmem],
        out_specs=(
            pl.BlockSpec((piece, rows), lambda i: (i, 0)),
            pl.BlockSpec((comps + 1, expos), lambda i: (0, 0)),
        ),
    )(total, summed)
    return (grad[None], params)


def solution(mesh):
    placed = (
        P("band", "tile", None),
        P("band", "tile", None, None),
        P("band", "tile", None),
        P("band", "tile", None, None),
        P("band", "tile", None),
        P("band", "tile"),
        P("band", "tile"),
        P(),
        P(),
        P(),
        P(),
    )
    return jax.shard_map(
        body, mesh=mesh, in_specs=placed, out_specs=(P("band", "tile", None), P()), check_vma=False
    )
```

```python
import functools

import jax
import jax.numpy as jnp
from jax import lax
from jax.experimental import pallas as pl
from jax.experimental.pallas import tpu as pltpu
from jax.sharding import PartitionSpec as P

MESH = pl.DeviceIdType.MESH
BF = jnp.bfloat16
F32 = jnp.float32
TN = (((0,), (0,)), ((), ()))
NT = (((1,), (1,)), ((), ()))


def iota(shape, dim):
    return lax.broadcasted_iota(jnp.int32, shape, dim)


def dot(a, b):
    return jnp.dot(a, b, preferred_element_type=F32)


def onehot(hit):
    return jnp.where(hit, 1.0, 0.0).astype(BF)


def spread(ref, expo):
    taps, comps, expos = ref.shape
    named = iota((comps, expos), 1) == expo
    lane = iota((comps, 256), 1) - (128 - taps // 2)
    straight = mirrored = jnp.zeros((comps, 256), F32)
    for t in range(taps):
        tap = jnp.sum(jnp.where(named, ref[t], 0.0), axis=1, keepdims=True)
        straight = jnp.where(lane == t, tap, straight)
        mirrored = jnp.where(lane == taps - 1 - t, tap, mirrored)
    return straight.astype(BF).astype(F32), mirrored.astype(BF).astype(F32)


def bands(base):
    x = jnp.concatenate([base] * 16, axis=0)
    row = iota(x.shape, 0)
    for bit in range(7):
        x = jnp.where((row & (1 << bit)) != 0, pltpu.roll(x, 1 << bit, 1), x)
    return x


def kernel(
    tiles,
    nband,
    cap,
    owner_ref,
    local_ref,
    weight_ref,
    offset_ref,
    expo_ref,
    amp_ref,
    frac_ref,
    sky_hbm,
    obs_hbm,
    col_hbm,
    rowp_hbm,
    total,
    summed_ref,
    sky,
    sky_t,
    obs,
    colp,
    rowp,
    hits,
    picks,
    req_out,
    req_in,
    rows_out,
    rows_in,
    grads_out,
    grads_in,
    card_out,
    cards,
    part_out,
    part_in,
    fet,
    resam,
    base,
    blur,
    fwd,
    bwd,
    tall,
    tall_t,
    obs_t,
    resid,
    back,
    adj,
    seg_grad,
    load_sem,
    req_s,
    req_r,
    rows_s,
    rows_r,
    grads_s,
    grads_r,
    cards_s,
    cards_r,
    part_s,
    part_r,
):
    me = lax.axis_index("tile")
    band = lax.axis_index("band")
    segs, rows = sky.shape
    width = obs.shape[0]
    comps = blur.shape[0]
    pixels = width * rows
    nblk = width // 256
    half = tiles // 2

    loads = [
        pltpu.make_async_copy(src, dst, load_sem.at[i])
        for i, (src, dst) in enumerate(
            ((sky_hbm, sky), (obs_hbm, obs), (col_hbm, colp), (rowp_hbm, rowp))
        )
    ]
    for load in loads:
        load.start()

    barrier = pltpu.get_barrier_semaphore()

    def loop(low, high, work):
        lax.fori_loop(low, high, lambda k, c: (work(k), c)[1], 0)

    loop(
        1,
        tiles,
        lambda k: pl.semaphore_signal(
            barrier, inc=1, device_id={"tile": lax.rem(me + k, tiles)}, device_id_type=MESH
        ),
    )
    loop(
        1,
        nband,
        lambda k: pl.semaphore_signal(
            barrier, inc=1, device_id={"band": lax.rem(band + k, nband)}, device_id_type=MESH
        ),
    )

    inner = lax.rem((me // max(1, tiles // 4) + 1) // 2, 2)

    def peer(step):
        pair = step // 2
        far = 1 - lax.rem(step + inner, 2)
        k = far * (half + pair) + (1 - far) * lax.rem(pair + 1, half)
        bits = [1 << b for b in range(tiles.bit_length() - 1)]
        return sum(lax.rem(me // bit + k // bit, 2) * bit for bit in bits)

    def push(src, dst, send, recv, p):
        return pltpu.make_async_remote_copy(
            src_ref=src.at[p],
            dst_ref=dst.at[me],
            send_sem=send.at[p],
            recv_sem=recv.at[me],
            device_id={"tile": p},
            device_id_type=MESH,
        )

    def arrival(src, dst, send, recv, p):
        return pltpu.make_async_remote_copy(
            src_ref=src.at[p],
            dst_ref=dst.at[p],
            send_sem=send.at[p],
            recv_sem=recv.at[p],
            device_id={"tile": p},
            device_id_type=MESH,
        )

    def deliver(src, dst, send, recv, p):
        @pl.when(p != me)
        def _():
            push(src, dst, send, recv, p).start()

        @pl.when(p == me)
        def _():
            dst[me] = src[me]

    def receive(src, dst, send, recv, p):
        @pl.when(p != me)
        def _():
            arrival(src, dst, send, recv, p).wait_recv()

    owner = owner_ref[...]
    member = jnp.where(iota((tiles, width), 0) == owner, 1.0, 0.0)
    pieces = [member[:, b * 128 : (b + 1) * 128] for b in range(width // 128)]
    above = onehot(iota((128, 128), 0) < iota((128, 128), 1))
    prefix = dot(jnp.concatenate(pieces, axis=0).astype(BF), above)
    run = jnp.zeros((tiles, 1), F32)
    ranks = []
    for b, piece in enumerate(pieces):
        earlier = prefix[b * tiles : (b + 1) * tiles] + run
        ranks.append(jnp.sum(piece * earlier, axis=0, keepdims=True))
        run = run + jnp.sum(piece, axis=1, keepdims=True)
    slot = owner * cap + jnp.concatenate(ranks, axis=1).astype(jnp.int32)
    wanted = local_ref[...] + 1
    which = iota((16, width), 0)
    digits = (
        jnp.where(which == 0, wanted >> 6, jnp.where(which == 1, wanted & 63, 0))
        .astype(F32)
        .astype(BF)
    )
    loads[0].wait()
    for b in range(segs // 128):
        sky_t[:, b * 128 : (b + 1) * 128] = sky[b * 128 : (b + 1) * 128, :].T

    pl.semaphore_wait(barrier, tiles - 1 + nband - 1)

    def ask(step):
        p = peer(step)
        hit = onehot(iota((cap, width), 0) + p * cap == slot)
        hits[p] = hit
        ids = lax.dot_general(digits, hit, NT, preferred_element_type=F32)
        req_out[p] = ids[0:1] * 64.0 + ids[1:2]
        deliver(req_out, req_in, req_s, req_r, p)

    loop(0, tiles, ask)

    keep = cap >= 128

    def pick(p):
        return onehot(iota((segs, cap), 0) + 1 == req_in[p].astype(jnp.int32))

    def serve(step):
        p = peer(step)
        receive(req_out, req_in, req_s, req_r, p)
        chosen = pick(p)
        if keep:
            picks[p] = chosen
        rows_out[p] = dot(sky_t[...], chosen).astype(BF)
        deliver(rows_out, rows_in, rows_s, rows_r, p)

    loop(0, tiles, serve)

    for load in loads[1:]:
        load.wait()
    expo = expo_ref[0, 0]
    offset = offset_ref[0, 0]
    amps = [amp_ref[q, expo] for q in range(comps)]
    for at, made in enumerate((*spread(colp, expo), *spread(rowp, expo))):
        for q in range(comps):
            base[at, q] = jnp.broadcast_to(made[q : q + 1], (8, 256))
    low = iota((128, 128), 1) < 64
    blank = jnp.zeros((128, 128), BF)

    def make_wide(at, wide):
        def work(q):
            made = bands(base[at, q])
            edge, mid = made[:, :128], made[:, 128:].astype(BF)
            left = jnp.where(low, 0.0, edge).astype(BF)
            right = jnp.where(low, edge, 0.0).astype(BF)
            for b, line in enumerate(((right, blank), (mid, right), (left, mid), (blank, left))):
                for h in range(2):
                    wide[q, b * 128 : (b + 1) * 128, h * 128 : (h + 1) * 128] = line[h]

        loop(0, comps, work)

    make_wide(1, fwd)
    make_wide(0, bwd)

    def make_tall(q):
        tall[q] = bands(base[2, q])[:, 128:].astype(BF)
        tall_t[q] = bands(base[3, q])[:, 128:].astype(BF)
        blur[q, :, :128] = blank
        blur[q, :, 128 + width :] = blank

    loop(0, comps, make_tall)
    resid[:, :128] = blank
    resid[:, 128 + width :] = blank
    for b in range(width // 128):
        obs_t[:, b * 128 : (b + 1) * 128] = obs[b * 128 : (b + 1) * 128, :].T
    heavy = jnp.broadcast_to(weight_ref[...], (128, 128)).T
    heavy = jnp.concatenate([heavy, heavy], axis=1)
    frac = jnp.full((128, 128), frac_ref[expo], F32)
    w_low = (1.0 - frac).astype(BF).astype(F32)
    w_high = frac.astype(BF).astype(F32)
    sub, lane = iota((128, 128), 0), iota((128, 128), 1)
    interp_t = (
        jnp.where(lane == sub + offset, w_low, 0.0)
        + jnp.where(lane == sub + offset + 1, w_high, 0.0)
    ).astype(BF)
    interp = (
        jnp.where(sub == lane + offset, w_low, 0.0)
        + jnp.where(sub == lane + offset + 1, w_high, 0.0)
    ).astype(BF)
    slope_t = (
        jnp.where(lane == sub + offset + 1, 1.0, 0.0) - jnp.where(lane == sub + offset, 1.0, 0.0)
    ).astype(BF)

    fet[...] = jnp.zeros_like(fet)

    def take(step):
        p = peer(step)
        receive(rows_out, rows_in, rows_s, rows_r, p)
        fet[...] += dot(rows_in[p], hits[p])

    loop(0, tiles, take)

    resam[...] = dot(interp_t, fet[...].astype(BF)).astype(BF)

    for q in range(comps):
        blur[q, :, 128 : 128 + width] = (amps[q] * dot(tall[q], resam[...])).astype(BF)

    for i in range(nblk):
        model = None
        for q in range(comps):
            part = dot(blur[q, :, i * 256 : i * 256 + 512], fwd[q])
            model = part if model is None else model + part
        weighted = heavy * (model - obs_t[:, i * 256 : (i + 1) * 256].astype(F32))
        resid[:, 128 + i * 256 : 384 + i * 256] = weighted.astype(BF)
    tall_all = jnp.concatenate([tall_t[q] for q in range(comps)], axis=1)
    for i in range(nblk):
        left = resid[:, i * 256 : i * 256 + 512]
        stack = []
        for q in range(comps):
            part = amps[q] * dot(left, bwd[q])
            back[q, :, i * 256 : (i + 1) * 256] = part
            stack.append(part.astype(BF))
        adjoint = dot(tall_all, jnp.concatenate(stack, axis=0))
        adj[:, i * 256 : (i + 1) * 256] = adjoint
        seg_grad[:, i * 256 : (i + 1) * 256] = dot(interp, adjoint.astype(BF)).astype(BF)

    def give(step):
        p = peer(step)
        sent = lax.dot_general(seg_grad[...], hits[p], NT, preferred_element_type=F32)
        grads_out[p] = sent.astype(BF)
        deliver(grads_out, grads_in, grads_s, grads_r, p)

    loop(0, half, give)

    terms = []
    for q in range(comps):
        acc = jnp.sum(blur[q, :, 128 : 128 + width].astype(F32) * back[q], axis=0, keepdims=True)
        gain = jnp.full((1, 1), amps[q], F32)
        terms.append(jnp.sum(acc, axis=1, keepdims=True) / (gain * gain * pixels))
    shift = jnp.sum(adj[...] * dot(slope_t, fet[...].astype(BF)), axis=0, keepdims=True)
    terms.append(jnp.sum(shift, axis=1, keepdims=True) / pixels)

    line = iota((8, 128), 0)
    card = jnp.where(line == 5, expo.astype(F32), 0.0)
    for q, term in enumerate(terms):
        card = jnp.where(line == q, jnp.broadcast_to(term, (8, 128)), card)
    card_out[...] = card
    cards[band] = card

    def swap(k, here):
        to = lax.rem(band + k, nband)
        return pltpu.make_async_remote_copy(
            src_ref=card_out,
            dst_ref=cards.at[band] if here else cards.at[to],
            send_sem=cards_s.at[to],
            recv_sem=cards_r.at[band] if here else cards_r.at[to],
            device_id={"band": to},
            device_id_type=MESH,
        )

    loop(1, nband, lambda k: swap(k, True).start())

    loop(half, tiles, give)

    loop(1, nband, lambda k: swap(k, False).wait_recv())
    expos = summed_ref.shape[1]
    column = iota((8, expos), 1).astype(F32)
    part = jnp.zeros((8, expos), F32)
    for b in range(nband):
        block = jnp.concatenate([cards[b]] * (expos // 128), axis=1)
        part = part + jnp.where(column == block[5:6, :], block, 0.0)
    part_out[...] = part
    part_in[me] = part

    def tell(k, here):
        p = lax.rem(me + k, tiles)
        return pltpu.make_async_remote_copy(
            src_ref=part_out,
            dst_ref=part_in.at[me] if here else part_in.at[p],
            send_sem=part_s.at[p],
            recv_sem=part_r.at[me] if here else part_r.at[p],
            device_id={"tile": p},
            device_id_type=MESH,
        )

    loop(1, tiles, lambda k: tell(k, True).start())

    total[...] = jnp.zeros_like(total)

    def collect(step):
        p = peer(step)
        receive(grads_out, grads_in, grads_s, grads_r, p)
        chosen = picks[p] if keep else pick(p)
        total[...] += lax.dot_general(chosen, grads_in[p], NT, preferred_element_type=F32)

    loop(0, tiles, collect)

    loop(1, tiles, lambda k: tell(k, False).wait_recv())
    summed_ref[...] = lax.fori_loop(
        0, tiles, lambda t, acc: acc + part_in[t], jnp.zeros((8, expos), F32)
    )

    def settle(k):
        p = lax.rem(me + k, tiles)
        push(req_out, req_in, req_s, req_r, p).wait_send()
        push(rows_out, rows_in, rows_s, rows_r, p).wait_send()
        push(grads_out, grads_in, grads_s, grads_r, p).wait_send()
        tell(k, True).wait_send()

    loop(1, tiles, settle)
    loop(1, nband, lambda k: swap(k, True).wait_send())


def finish(total, summed, grad_ref, params_ref, sem):
    pieces = sem.shape[0]
    size = total.shape[0] // pieces
    moves = [
        pltpu.make_async_copy(
            total.at[pl.ds(i * size, size)], grad_ref.at[pl.ds(i * size, size)], sem.at[i]
        )
        for i in range(pieces)
    ]
    for move in moves:
        move.start()
    params_ref[...] = summed[: params_ref.shape[0]]
    for move in moves:
        move.wait()


def body(
    sky_model,
    observed,
    row_weight,
    foot_owner,
    foot_local,
    row_offset,
    exposure_of,
    amplitude,
    subpixel_shift,
    column_profile,
    row_profile,
):
    tiles = lax.axis_size("tile")
    nband = lax.axis_size("band")
    segs, rows = sky_model.shape[1:]
    width = observed.shape[2]
    comps, expos = amplitude.shape
    taps = column_profile.shape[2]
    cap = 2 * width // tiles
    vmem = pl.BlockSpec(memory_space=pltpu.VMEM)
    smem = pl.BlockSpec(memory_space=pltpu.SMEM)
    hbm = pl.BlockSpec(memory_space=pltpu.HBM)
    dma = pltpu.SemaphoreType.DMA
    total, summed = pl.pallas_call(
        functools.partial(kernel, tiles, nband, cap),
        out_shape=(
            jax.ShapeDtypeStruct((segs, rows), F32),
            jax.ShapeDtypeStruct((8, expos), F32),
        ),
        in_specs=[vmem, vmem, vmem, smem, smem, smem, smem, hbm, hbm, hbm, hbm],
        out_specs=(vmem, vmem),
        scratch_shapes=[
            pltpu.VMEM((segs, rows), BF),
            pltpu.VMEM((rows, segs), BF),
            pltpu.VMEM((width, rows), BF),
            pltpu.VMEM((taps, comps, expos), F32),
            pltpu.VMEM((taps, comps, expos), F32),
            pltpu.VMEM((tiles, cap, width), BF),
            pltpu.VMEM((tiles, segs, cap) if cap >= 128 else (16, 128), BF),
            pltpu.VMEM((tiles, 1, cap), F32),
            pltpu.VMEM((tiles, 1, cap), F32),
            pltpu.VMEM((tiles, rows, cap), BF),
            pltpu.VMEM((tiles, rows, cap), BF),
            pltpu.VMEM((tiles, rows, cap), BF),
            pltpu.VMEM((tiles, rows, cap), BF),
            pltpu.VMEM((8, 128), F32),
            pltpu.VMEM((nband, 8, 128), F32),
            pltpu.VMEM((8, expos), F32),
            pltpu.VMEM((tiles, 8, expos), F32),
            pltpu.VMEM((rows, width), F32),
            pltpu.VMEM((rows, width), BF),
            pltpu.VMEM((4, comps, 8, 256), F32),
            pltpu.VMEM((comps, rows, width + 256), BF),
            pltpu.VMEM((comps, 512, 256), BF),
            pltpu.VMEM((comps, 512, 256), BF),
            pltpu.VMEM((comps, rows, rows), BF),
            pltpu.VMEM((comps, rows, rows), BF),
            pltpu.VMEM((rows, width), BF),
            pltpu.VMEM((rows, width + 256), BF),
            pltpu.VMEM((comps, rows, width), F32),
            pltpu.VMEM((rows, width), F32),
            pltpu.VMEM((rows, width), BF),
            dma((4,)),
        ]
        + [dma((tiles,))] * 6
        + [dma((nband,))] * 2
        + [dma((tiles,))] * 2,
        compiler_params=pltpu.CompilerParams(
            collective_id=0, has_side_effects=True, vmem_limit_bytes=60 * 1024 * 1024
        ),
    )(
        foot_owner.reshape(1, width),
        foot_local.reshape(1, width),
        row_weight.reshape(1, rows),
        row_offset,
        exposure_of,
        amplitude,
        subpixel_shift,
        sky_model[0],
        observed[0, 0],
        column_profile.transpose(2, 1, 0),
        row_profile.transpose(2, 1, 0),
    )
    grad, params = pl.pallas_call(
        finish,
        out_shape=(
            jax.ShapeDtypeStruct((segs, rows), F32),
            jax.ShapeDtypeStruct((comps + 1, expos), F32),
        ),
        in_specs=[hbm, vmem],
        out_specs=(hbm, vmem),
        scratch_shapes=[dma((8,))],
        compiler_params=pltpu.CompilerParams(vmem_limit_bytes=60 * 1024 * 1024),
    )(total, summed)
    return (grad[None], params)


def solution(mesh):
    placed = (
        P("band", "tile", None),
        P("band", "tile", None, None),
        P("band", "tile", None),
        P("band", "tile", None, None),
        P("band", "tile", None),
        P("band", "tile"),
        P("band", "tile"),
        P(),
        P(),
        P(),
        P(),
    )
    return jax.shard_map(
        body, mesh=mesh, in_specs=placed, out_specs=(P("band", "tile", None), P()), check_vma=False
    )
```

```python
import functools

import jax
import jax.numpy as jnp
from jax import lax
from jax.experimental import pallas as pl
from jax.experimental.pallas import tpu as pltpu
from jax.sharding import PartitionSpec as P

MESH = pl.DeviceIdType.MESH
BF = jnp.bfloat16
F32 = jnp.float32
TN = (((0,), (0,)), ((), ()))
NT = (((1,), (1,)), ((), ()))


def iota(shape, dim):
    return lax.broadcasted_iota(jnp.int32, shape, dim)


def dot(a, b):
    return jnp.dot(a, b, preferred_element_type=F32)


def onehot(hit):
    return jnp.where(hit, 1.0, 0.0).astype(BF)


def spread(ref, expo):
    taps, comps, expos = ref.shape
    named = iota((comps, expos), 1) == expo
    lane = iota((comps, 256), 1) - (128 - taps // 2)
    straight = mirrored = jnp.zeros((comps, 256), F32)
    for t in range(taps):
        tap = jnp.sum(jnp.where(named, ref[t], 0.0), axis=1, keepdims=True)
        straight = jnp.where(lane == t, tap, straight)
        mirrored = jnp.where(lane == taps - 1 - t, tap, mirrored)
    return straight.astype(BF).astype(F32), mirrored.astype(BF).astype(F32)


def bands(base):
    x = jnp.concatenate([base] * 16, axis=0)
    row = iota(x.shape, 0)
    for bit in range(7):
        x = jnp.where((row & (1 << bit)) != 0, pltpu.roll(x, 1 << bit, 1), x)
    return x


def kernel(
    tiles,
    nband,
    cap,
    owner_ref,
    local_ref,
    weight_ref,
    offset_ref,
    expo_ref,
    amp_ref,
    frac_ref,
    sky_hbm,
    obs_hbm,
    col_hbm,
    rowp_hbm,
    total,
    summed_ref,
    sky,
    sky_t,
    obs,
    colp,
    rowp,
    hits,
    picks,
    req_out,
    req_in,
    rows_out,
    rows_in,
    grads_out,
    grads_in,
    card_out,
    cards,
    part_out,
    part_in,
    fet,
    resam,
    base,
    blur,
    fwd,
    bwd,
    tall,
    tall_t,
    obs_t,
    resid,
    back,
    adj,
    seg_grad,
    load_sem,
    req_s,
    req_r,
    rows_s,
    rows_r,
    grads_s,
    grads_r,
    cards_s,
    cards_r,
    part_s,
    part_r,
):
    me = lax.axis_index("tile")
    band = lax.axis_index("band")
    segs, rows = sky.shape
    width = obs.shape[0]
    comps = blur.shape[0]
    pixels = width * rows
    nblk = width // 256
    half = tiles // 2

    loads = [
        pltpu.make_async_copy(src, dst, load_sem.at[i])
        for i, (src, dst) in enumerate(
            ((sky_hbm, sky), (obs_hbm, obs), (col_hbm, colp), (rowp_hbm, rowp))
        )
    ]
    for load in loads:
        load.start()

    barrier = pltpu.get_barrier_semaphore()

    def loop(low, high, work):
        lax.fori_loop(low, high, lambda k, c: (work(k), c)[1], 0)

    loop(
        1,
        tiles,
        lambda k: pl.semaphore_signal(
            barrier, inc=1, device_id={"tile": lax.rem(me + k, tiles)}, device_id_type=MESH
        ),
    )
    loop(
        1,
        nband,
        lambda k: pl.semaphore_signal(
            barrier, inc=1, device_id={"band": lax.rem(band + k, nband)}, device_id_type=MESH
        ),
    )

    inner = lax.rem((me // max(1, tiles // 4) + 1) // 2, 2)

    def peer(step):
        pair = step // 2
        far = 1 - lax.rem(step + inner, 2)
        k = far * (half + pair) + (1 - far) * lax.rem(pair + 1, half)
        bits = [1 << b for b in range(tiles.bit_length() - 1)]
        return sum(lax.rem(me // bit + k // bit, 2) * bit for bit in bits)

    def push(src, dst, send, recv, p):
        return pltpu.make_async_remote_copy(
            src_ref=src.at[p],
            dst_ref=dst.at[me],
            send_sem=send.at[p],
            recv_sem=recv.at[me],
            device_id={"tile": p},
            device_id_type=MESH,
        )

    def arrival(src, dst, send, recv, p):
        return pltpu.make_async_remote_copy(
            src_ref=src.at[p],
            dst_ref=dst.at[p],
            send_sem=send.at[p],
            recv_sem=recv.at[p],
            device_id={"tile": p},
            device_id_type=MESH,
        )

    def deliver(src, dst, send, recv, p):
        @pl.when(p != me)
        def _():
            push(src, dst, send, recv, p).start()

        @pl.when(p == me)
        def _():
            dst[me] = src[me]

    def receive(src, dst, send, recv, p):
        @pl.when(p != me)
        def _():
            arrival(src, dst, send, recv, p).wait_recv()

    owner = owner_ref[...]
    member = jnp.where(iota((tiles, width), 0) == owner, 1.0, 0.0)
    pieces = [member[:, b * 128 : (b + 1) * 128] for b in range(width // 128)]
    above = onehot(iota((128, 128), 0) < iota((128, 128), 1))
    prefix = dot(jnp.concatenate(pieces, axis=0).astype(BF), above)
    run = jnp.zeros((tiles, 1), F32)
    ranks = []
    for b, piece in enumerate(pieces):
        earlier = prefix[b * tiles : (b + 1) * tiles] + run
        ranks.append(jnp.sum(piece * earlier, axis=0, keepdims=True))
        run = run + jnp.sum(piece, axis=1, keepdims=True)
    slot = owner * cap + jnp.concatenate(ranks, axis=1).astype(jnp.int32)
    wanted = local_ref[...] + 1
    which = iota((16, width), 0)
    digits = (
        jnp.where(which == 0, wanted >> 6, jnp.where(which == 1, wanted & 63, 0))
        .astype(F32)
        .astype(BF)
    )
    pl.semaphore_wait(barrier, tiles - 1 + nband - 1)

    def ask(step):
        p = peer(step)
        hit = onehot(iota((cap, width), 0) + p * cap == slot)
        hits[p] = hit
        ids = lax.dot_general(digits, hit, NT, preferred_element_type=F32)
        req_out[p] = ids[0:1] * 64.0 + ids[1:2]
        deliver(req_out, req_in, req_s, req_r, p)

    loop(0, half, ask)
    loads[0].wait()
    for b in range(segs // 128):
        sky_t[:, b * 128 : (b + 1) * 128] = sky[b * 128 : (b + 1) * 128, :].T

    keep = cap >= 128

    def pick(p):
        return onehot(iota((segs, cap), 0) + 1 == req_in[p].astype(jnp.int32))

    def serve(step):
        p = peer(step)
        receive(req_out, req_in, req_s, req_r, p)
        chosen = pick(p)
        if keep:
            picks[p] = chosen
        rows_out[p] = dot(sky_t[...], chosen).astype(BF)
        deliver(rows_out, rows_in, rows_s, rows_r, p)

    def both(step):
        serve(step)
        ask(step + half)

    loop(0, half, both)
    loop(half, tiles, serve)

    for load in loads[1:]:
        load.wait()
    expo = expo_ref[0, 0]
    offset = offset_ref[0, 0]
    amps = [amp_ref[q, expo] for q in range(comps)]
    for at, made in enumerate((*spread(colp, expo), *spread(rowp, expo))):
        for q in range(comps):
            base[at, q] = jnp.broadcast_to(made[q : q + 1], (8, 256))
    low = iota((128, 128), 1) < 64
    blank = jnp.zeros((128, 128), BF)

    def make_wide(at, wide):
        def work(q):
            made = bands(base[at, q])
            edge, mid = made[:, :128], made[:, 128:].astype(BF)
            left = jnp.where(low, 0.0, edge).astype(BF)
            right = jnp.where(low, edge, 0.0).astype(BF)
            for b, line in enumerate(((right, blank), (mid, right), (left, mid), (blank, left))):
                for h in range(2):
                    wide[q, b * 128 : (b + 1) * 128, h * 128 : (h + 1) * 128] = line[h]

        loop(0, comps, work)

    make_wide(1, fwd)
    make_wide(0, bwd)

    def make_tall(q):
        tall[q] = bands(base[2, q])[:, 128:].astype(BF)
        tall_t[q] = bands(base[3, q])[:, 128:].astype(BF)
        blur[q, :, :128] = blank
        blur[q, :, 128 + width :] = blank

    loop(0, comps, make_tall)
    resid[:, :128] = blank
    resid[:, 128 + width :] = blank
    for b in range(width // 128):
        obs_t[:, b * 128 : (b + 1) * 128] = obs[b * 128 : (b + 1) * 128, :].T
    heavy = jnp.broadcast_to(weight_ref[...], (128, 128)).T
    heavy = jnp.concatenate([heavy, heavy], axis=1)
    frac = jnp.full((128, 128), frac_ref[expo], F32)
    w_low = (1.0 - frac).astype(BF).astype(F32)
    w_high = frac.astype(BF).astype(F32)
    sub, lane = iota((128, 128), 0), iota((128, 128), 1)
    interp_t = (
        jnp.where(lane == sub + offset, w_low, 0.0)
        + jnp.where(lane == sub + offset + 1, w_high, 0.0)
    ).astype(BF)
    interp = (
        jnp.where(sub == lane + offset, w_low, 0.0)
        + jnp.where(sub == lane + offset + 1, w_high, 0.0)
    ).astype(BF)
    slope_t = (
        jnp.where(lane == sub + offset + 1, 1.0, 0.0) - jnp.where(lane == sub + offset, 1.0, 0.0)
    ).astype(BF)

    fet[...] = jnp.zeros_like(fet)

    def take(step):
        p = peer(step)
        receive(rows_out, rows_in, rows_s, rows_r, p)
        fet[...] += dot(rows_in[p], hits[p])

    loop(0, tiles, take)

    resam[...] = dot(interp_t, fet[...].astype(BF)).astype(BF)

    tall_rows = jnp.concatenate([tall[q] for q in range(comps)], axis=0)
    for i in range(nblk):
        part = dot(tall_rows, resam[:, i * 256 : (i + 1) * 256])
        for q in range(comps):
            blur[q, :, 128 + i * 256 : 384 + i * 256] = (
                amps[q] * part[q * 128 : (q + 1) * 128]
            ).astype(BF)

    for i in range(nblk):
        model = None
        for q in range(comps):
            part = dot(blur[q, :, i * 256 : i * 256 + 512], fwd[q])
            model = part if model is None else model + part
        weighted = heavy * (model - obs_t[:, i * 256 : (i + 1) * 256].astype(F32))
        resid[:, 128 + i * 256 : 384 + i * 256] = weighted.astype(BF)
    tall_all = jnp.concatenate([tall_t[q] for q in range(comps)], axis=1)
    for i in range(nblk):
        left = resid[:, i * 256 : i * 256 + 512]
        stack = []
        for q in range(comps):
            part = amps[q] * dot(left, bwd[q])
            back[q, :, i * 256 : (i + 1) * 256] = part
            stack.append(part.astype(BF))
        adjoint = dot(tall_all, jnp.concatenate(stack, axis=0))
        adj[:, i * 256 : (i + 1) * 256] = adjoint
        seg_grad[:, i * 256 : (i + 1) * 256] = dot(interp, adjoint.astype(BF)).astype(BF)

    def give(step):
        p = peer(step)
        sent = lax.dot_general(seg_grad[...], hits[p], NT, preferred_element_type=F32)
        grads_out[p] = sent.astype(BF)
        deliver(grads_out, grads_in, grads_s, grads_r, p)

    loop(0, half, give)

    terms = []
    for q in range(comps):
        acc = jnp.sum(blur[q, :, 128 : 128 + width].astype(F32) * back[q], axis=0, keepdims=True)
        gain = jnp.full((1, 1), amps[q], F32)
        terms.append(jnp.sum(acc, axis=1, keepdims=True) / (gain * gain * pixels))
    shift = jnp.sum(adj[...] * dot(slope_t, fet[...].astype(BF)), axis=0, keepdims=True)
    terms.append(jnp.sum(shift, axis=1, keepdims=True) / pixels)

    line = iota((8, 128), 0)
    card = jnp.where(line == 5, expo.astype(F32), 0.0)
    for q, term in enumerate(terms):
        card = jnp.where(line == q, jnp.broadcast_to(term, (8, 128)), card)
    card_out[...] = card
    cards[band] = card

    def swap(k, here):
        to = lax.rem(band + k, nband)
        return pltpu.make_async_remote_copy(
            src_ref=card_out,
            dst_ref=cards.at[band] if here else cards.at[to],
            send_sem=cards_s.at[to],
            recv_sem=cards_r.at[band] if here else cards_r.at[to],
            device_id={"band": to},
            device_id_type=MESH,
        )

    loop(1, nband, lambda k: swap(k, True).start())

    loop(half, tiles, give)

    loop(1, nband, lambda k: swap(k, False).wait_recv())
    expos = summed_ref.shape[1]
    column = iota((8, expos), 1).astype(F32)
    part = jnp.zeros((8, expos), F32)
    for b in range(nband):
        block = jnp.concatenate([cards[b]] * (expos // 128), axis=1)
        part = part + jnp.where(column == block[5:6, :], block, 0.0)
    part_out[...] = part
    part_in[me] = part

    def tell(k, here):
        p = lax.rem(me + k, tiles)
        return pltpu.make_async_remote_copy(
            src_ref=part_out,
            dst_ref=part_in.at[me] if here else part_in.at[p],
            send_sem=part_s.at[p],
            recv_sem=part_r.at[me] if here else part_r.at[p],
            device_id={"tile": p},
            device_id_type=MESH,
        )

    loop(1, tiles, lambda k: tell(k, True).start())

    total[...] = jnp.zeros_like(total)

    def collect(step):
        p = peer(step)
        receive(grads_out, grads_in, grads_s, grads_r, p)
        chosen = picks[p] if keep else pick(p)
        total[...] += lax.dot_general(chosen, grads_in[p], NT, preferred_element_type=F32)

    loop(0, tiles, collect)

    loop(1, tiles, lambda k: tell(k, False).wait_recv())
    summed_ref[...] = lax.fori_loop(
        0, tiles, lambda t, acc: acc + part_in[t], jnp.zeros((8, expos), F32)
    )

    def settle(k):
        p = lax.rem(me + k, tiles)
        push(req_out, req_in, req_s, req_r, p).wait_send()
        push(rows_out, rows_in, rows_s, rows_r, p).wait_send()
        push(grads_out, grads_in, grads_s, grads_r, p).wait_send()
        tell(k, True).wait_send()

    loop(1, tiles, settle)
    loop(1, nband, lambda k: swap(k, True).wait_send())


def finish(total, summed, grad_ref, params_ref, held, in_sem, out_sem):
    pieces = in_sem.shape[0]
    size = total.shape[0] // pieces
    spans = [pl.ds(i * size, size) for i in range(pieces)]
    reads = [
        pltpu.make_async_copy(total.at[at], held.at[at], in_sem.at[i])
        for i, at in enumerate(spans)
    ]
    writes = [
        pltpu.make_async_copy(held.at[at], grad_ref.at[at], out_sem.at[i])
        for i, at in enumerate(spans)
    ]
    for read in reads:
        read.start()
    params_ref[...] = summed[: params_ref.shape[0]]
    for read, write in zip(reads, writes):
        read.wait()
        write.start()
    for write in writes:
        write.wait()


def body(
    sky_model,
    observed,
    row_weight,
    foot_owner,
    foot_local,
    row_offset,
    exposure_of,
    amplitude,
    subpixel_shift,
    column_profile,
    row_profile,
):
    tiles = lax.axis_size("tile")
    nband = lax.axis_size("band")
    segs, rows = sky_model.shape[1:]
    width = observed.shape[2]
    comps, expos = amplitude.shape
    taps = column_profile.shape[2]
    cap = 2 * width // tiles
    vmem = pl.BlockSpec(memory_space=pltpu.VMEM)
    smem = pl.BlockSpec(memory_space=pltpu.SMEM)
    hbm = pl.BlockSpec(memory_space=pltpu.HBM)
    dma = pltpu.SemaphoreType.DMA
    total, summed = pl.pallas_call(
        functools.partial(kernel, tiles, nband, cap),
        out_shape=(
            jax.ShapeDtypeStruct((segs, rows), F32),
            jax.ShapeDtypeStruct((8, expos), F32),
        ),
        in_specs=[vmem, vmem, vmem, smem, smem, smem, smem, hbm, hbm, hbm, hbm],
        out_specs=(vmem, vmem),
        scratch_shapes=[
            pltpu.VMEM((segs, rows), BF),
            pltpu.VMEM((rows, segs), BF),
            pltpu.VMEM((width, rows), BF),
            pltpu.VMEM((taps, comps, expos), F32),
            pltpu.VMEM((taps, comps, expos), F32),
            pltpu.VMEM((tiles, cap, width), BF),
            pltpu.VMEM((tiles, segs, cap) if cap >= 128 else (16, 128), BF),
            pltpu.VMEM((tiles, 1, cap), F32),
            pltpu.VMEM((tiles, 1, cap), F32),
            pltpu.VMEM((tiles, rows, cap), BF),
            pltpu.VMEM((tiles, rows, cap), BF),
            pltpu.VMEM((tiles, rows, cap), BF),
            pltpu.VMEM((tiles, rows, cap), BF),
            pltpu.VMEM((8, 128), F32),
            pltpu.VMEM((nband, 8, 128), F32),
            pltpu.VMEM((8, expos), F32),
            pltpu.VMEM((tiles, 8, expos), F32),
            pltpu.VMEM((rows, width), F32),
            pltpu.VMEM((rows, width), BF),
            pltpu.VMEM((4, comps, 8, 256), F32),
            pltpu.VMEM((comps, rows, width + 256), BF),
            pltpu.VMEM((comps, 512, 256), BF),
            pltpu.VMEM((comps, 512, 256), BF),
            pltpu.VMEM((comps, rows, rows), BF),
            pltpu.VMEM((comps, rows, rows), BF),
            pltpu.VMEM((rows, width), BF),
            pltpu.VMEM((rows, width + 256), BF),
            pltpu.VMEM((comps, rows, width), F32),
            pltpu.VMEM((rows, width), F32),
            pltpu.VMEM((rows, width), BF),
            dma((4,)),
        ]
        + [dma((tiles,))] * 6
        + [dma((nband,))] * 2
        + [dma((tiles,))] * 2,
        compiler_params=pltpu.CompilerParams(
            collective_id=0, has_side_effects=True, vmem_limit_bytes=60 * 1024 * 1024
        ),
    )(
        foot_owner.reshape(1, width),
        foot_local.reshape(1, width),
        row_weight.reshape(1, rows),
        row_offset,
        exposure_of,
        amplitude,
        subpixel_shift,
        sky_model[0],
        observed[0, 0],
        column_profile.transpose(2, 1, 0),
        row_profile.transpose(2, 1, 0),
    )
    grad, params = pl.pallas_call(
        finish,
        out_shape=(
            jax.ShapeDtypeStruct((segs, rows), F32),
            jax.ShapeDtypeStruct((comps + 1, expos), F32),
        ),
        in_specs=[hbm, vmem],
        out_specs=(hbm, vmem),
        scratch_shapes=[pltpu.VMEM((segs, rows), F32), dma((8,)), dma((8,))],
        compiler_params=pltpu.CompilerParams(vmem_limit_bytes=60 * 1024 * 1024),
    )(total, summed)
    return (grad[None], params)


def solution(mesh):
    placed = (
        P("band", "tile", None),
        P("band", "tile", None, None),
        P("band", "tile", None),
        P("band", "tile", None, None),
        P("band", "tile", None),
        P("band", "tile"),
        P("band", "tile"),
        P(),
        P(),
        P(),
        P(),
    )
    return jax.shard_map(
        body, mesh=mesh, in_specs=placed, out_specs=(P("band", "tile", None), P()), check_vma=False
    )
```

```python
import functools

import jax
import jax.numpy as jnp
from jax import lax
from jax.experimental import pallas as pl
from jax.experimental.pallas import tpu as pltpu
from jax.sharding import PartitionSpec as P

MESH = pl.DeviceIdType.MESH
BF = jnp.bfloat16
F32 = jnp.float32
TN = (((0,), (0,)), ((), ()))
NT = (((1,), (1,)), ((), ()))


def iota(shape, dim):
    return lax.broadcasted_iota(jnp.int32, shape, dim)


def dot(a, b):
    return jnp.dot(a, b, preferred_element_type=F32)


def onehot(hit):
    return jnp.where(hit, 1.0, 0.0).astype(BF)


def spread(ref, expo):
    taps, comps, expos = ref.shape
    named = iota((comps, expos), 1) == expo
    lane = iota((comps, 256), 1) - (128 - taps // 2)
    straight = mirrored = jnp.zeros((comps, 256), F32)
    for t in range(taps):
        tap = jnp.sum(jnp.where(named, ref[t], 0.0), axis=1, keepdims=True)
        straight = jnp.where(lane == t, tap, straight)
        mirrored = jnp.where(lane == taps - 1 - t, tap, mirrored)
    return straight.astype(BF).astype(F32), mirrored.astype(BF).astype(F32)


def bands(base):
    x = jnp.concatenate([base] * 16, axis=0)
    row = iota(x.shape, 0)
    for bit in range(7):
        x = jnp.where((row & (1 << bit)) != 0, pltpu.roll(x, 1 << bit, 1), x)
    return x


def kernel(
    tiles,
    nband,
    cap,
    owner_ref,
    local_ref,
    weight_ref,
    offset_ref,
    expo_ref,
    amp_ref,
    frac_ref,
    sky_hbm,
    obs_hbm,
    col_hbm,
    rowp_hbm,
    total,
    summed_ref,
    sky,
    sky_t,
    obs,
    colp,
    rowp,
    hits,
    picks,
    req_out,
    req_in,
    rows_out,
    rows_in,
    grads_out,
    grads_in,
    card_out,
    cards,
    part_out,
    part_in,
    fet,
    resam,
    base,
    blur,
    fwd,
    bwd,
    tall,
    tall_t,
    obs_t,
    resid,
    back,
    adj,
    seg_grad,
    load_sem,
    req_s,
    req_r,
    rows_s,
    rows_r,
    grads_s,
    grads_r,
    cards_s,
    cards_r,
    part_s,
    part_r,
):
    me = lax.axis_index("tile")
    band = lax.axis_index("band")
    segs, rows = sky.shape
    width = obs.shape[0]
    comps = blur.shape[0]
    pixels = width * rows
    nblk = width // 256
    half = tiles // 2

    loads = [
        pltpu.make_async_copy(src, dst, load_sem.at[i])
        for i, (src, dst) in enumerate(
            ((sky_hbm, sky), (obs_hbm, obs), (col_hbm, colp), (rowp_hbm, rowp))
        )
    ]
    for load in loads:
        load.start()

    barrier = pltpu.get_barrier_semaphore()

    def loop(low, high, work):
        lax.fori_loop(low, high, lambda k, c: (work(k), c)[1], 0)

    loop(
        1,
        tiles,
        lambda k: pl.semaphore_signal(
            barrier, inc=1, device_id={"tile": lax.rem(me + k, tiles)}, device_id_type=MESH
        ),
    )
    loop(
        1,
        nband,
        lambda k: pl.semaphore_signal(
            barrier, inc=1, device_id={"band": lax.rem(band + k, nband)}, device_id_type=MESH
        ),
    )

    def after(step):
        return lax.rem(me + 1 + step, tiles)

    def ahead(step):
        return lax.rem(me + 2 * tiles - 1 - step, tiles)

    def push(src, dst, send, recv, p):
        return pltpu.make_async_remote_copy(
            src_ref=src.at[p],
            dst_ref=dst.at[me],
            send_sem=send.at[p],
            recv_sem=recv.at[me],
            device_id={"tile": p},
            device_id_type=MESH,
        )

    def arrival(src, dst, send, recv, p):
        return pltpu.make_async_remote_copy(
            src_ref=src.at[p],
            dst_ref=dst.at[p],
            send_sem=send.at[p],
            recv_sem=recv.at[p],
            device_id={"tile": p},
            device_id_type=MESH,
        )

    def deliver(src, dst, send, recv, p):
        @pl.when(p != me)
        def _():
            push(src, dst, send, recv, p).start()

        @pl.when(p == me)
        def _():
            dst[me] = src[me]

    def receive(src, dst, send, recv, p):
        @pl.when(p != me)
        def _():
            arrival(src, dst, send, recv, p).wait_recv()

    owner = owner_ref[...]
    member = jnp.where(iota((tiles, width), 0) == owner, 1.0, 0.0)
    pieces = [member[:, b * 128 : (b + 1) * 128] for b in range(width // 128)]
    above = onehot(iota((128, 128), 0) < iota((128, 128), 1))
    prefix = dot(jnp.concatenate(pieces, axis=0).astype(BF), above)
    run = jnp.zeros((tiles, 1), F32)
    ranks = []
    for b, piece in enumerate(pieces):
        earlier = prefix[b * tiles : (b + 1) * tiles] + run
        ranks.append(jnp.sum(piece * earlier, axis=0, keepdims=True))
        run = run + jnp.sum(piece, axis=1, keepdims=True)
    slot = owner * cap + jnp.concatenate(ranks, axis=1).astype(jnp.int32)
    wanted = local_ref[...] + 1
    which = iota((16, width), 0)
    digits = (
        jnp.where(which == 0, wanted >> 6, jnp.where(which == 1, wanted & 63, 0))
        .astype(F32)
        .astype(BF)
    )
    pl.semaphore_wait(barrier, tiles - 1 + nband - 1)

    def ask(step):
        p = after(step)
        hit = onehot(iota((cap, width), 0) + p * cap == slot)
        hits[p] = hit
        ids = lax.dot_general(digits, hit, NT, preferred_element_type=F32)
        req_out[p] = ids[0:1] * 64.0 + ids[1:2]
        deliver(req_out, req_in, req_s, req_r, p)

    loop(0, tiles, ask)
    loads[0].wait()
    for b in range(segs // 128):
        sky_t[:, b * 128 : (b + 1) * 128] = sky[b * 128 : (b + 1) * 128, :].T

    keep = cap >= 128

    def pick(p):
        return onehot(iota((segs, cap), 0) + 1 == req_in[p].astype(jnp.int32))

    def serve(step):
        p = ahead(step)
        receive(req_out, req_in, req_s, req_r, p)
        chosen = pick(p)
        if keep:
            picks[p] = chosen
        rows_out[p] = dot(sky_t[...], chosen).astype(BF)
        deliver(rows_out, rows_in, rows_s, rows_r, p)

    loop(0, tiles, serve)

    for load in loads[1:]:
        load.wait()
    expo = expo_ref[0, 0]
    offset = offset_ref[0, 0]
    amps = [amp_ref[q, expo] for q in range(comps)]
    for at, made in enumerate((*spread(colp, expo), *spread(rowp, expo))):
        for q in range(comps):
            base[at, q] = jnp.broadcast_to(made[q : q + 1], (8, 256))
    low = iota((128, 128), 1) < 64
    blank = jnp.zeros((128, 128), BF)

    def make_wide(at, wide):
        def work(q):
            made = bands(base[at, q])
            edge, mid = made[:, :128], made[:, 128:].astype(BF)
            left = jnp.where(low, 0.0, edge).astype(BF)
            right = jnp.where(low, edge, 0.0).astype(BF)
            for b, line in enumerate(((right, blank), (mid, right), (left, mid), (blank, left))):
                for h in range(2):
                    wide[q, b * 128 : (b + 1) * 128, h * 128 : (h + 1) * 128] = line[h]

        loop(0, comps, work)

    make_wide(1, fwd)
    make_wide(0, bwd)

    def make_tall(q):
        tall[q] = bands(base[2, q])[:, 128:].astype(BF)
        tall_t[q] = bands(base[3, q])[:, 128:].astype(BF)
        blur[q, :, :128] = blank
        blur[q, :, 128 + width :] = blank

    loop(0, comps, make_tall)
    resid[:, :128] = blank
    resid[:, 128 + width :] = blank
    for b in range(width // 128):
        obs_t[:, b * 128 : (b + 1) * 128] = obs[b * 128 : (b + 1) * 128, :].T
    heavy = jnp.broadcast_to(weight_ref[...], (128, 128)).T
    heavy = jnp.concatenate([heavy, heavy], axis=1)
    frac = jnp.full((128, 128), frac_ref[expo], F32)
    w_low = (1.0 - frac).astype(BF).astype(F32)
    w_high = frac.astype(BF).astype(F32)
    sub, lane = iota((128, 128), 0), iota((128, 128), 1)
    interp_t = (
        jnp.where(lane == sub + offset, w_low, 0.0)
        + jnp.where(lane == sub + offset + 1, w_high, 0.0)
    ).astype(BF)
    interp = (
        jnp.where(sub == lane + offset, w_low, 0.0)
        + jnp.where(sub == lane + offset + 1, w_high, 0.0)
    ).astype(BF)
    slope_t = (
        jnp.where(lane == sub + offset + 1, 1.0, 0.0) - jnp.where(lane == sub + offset, 1.0, 0.0)
    ).astype(BF)

    fet[...] = jnp.zeros_like(fet)

    def take(step):
        p = after(step)
        receive(rows_out, rows_in, rows_s, rows_r, p)
        fet[...] += dot(rows_in[p], hits[p])

    loop(0, tiles, take)

    resam[...] = dot(interp_t, fet[...].astype(BF)).astype(BF)

    tall_rows = jnp.concatenate([tall[q] for q in range(comps)], axis=0)
    for i in range(nblk):
        part = dot(tall_rows, resam[:, i * 256 : (i + 1) * 256])
        for q in range(comps):
            blur[q, :, 128 + i * 256 : 384 + i * 256] = (
                amps[q] * part[q * 128 : (q + 1) * 128]
            ).astype(BF)

    for i in range(nblk):
        model = None
        for q in range(comps):
            part = dot(blur[q, :, i * 256 : i * 256 + 512], fwd[q])
            model = part if model is None else model + part
        weighted = heavy * (model - obs_t[:, i * 256 : (i + 1) * 256].astype(F32))
        resid[:, 128 + i * 256 : 384 + i * 256] = weighted.astype(BF)
    tall_all = jnp.concatenate([tall_t[q] for q in range(comps)], axis=1)
    for i in range(nblk):
        left = resid[:, i * 256 : i * 256 + 512]
        stack = []
        for q in range(comps):
            part = amps[q] * dot(left, bwd[q])
            back[q, :, i * 256 : (i + 1) * 256] = part
            stack.append(part.astype(BF))
        adjoint = dot(tall_all, jnp.concatenate(stack, axis=0))
        adj[:, i * 256 : (i + 1) * 256] = adjoint
        seg_grad[:, i * 256 : (i + 1) * 256] = dot(interp, adjoint.astype(BF)).astype(BF)

    def give(step):
        p = after(step)
        sent = lax.dot_general(seg_grad[...], hits[p], NT, preferred_element_type=F32)
        grads_out[p] = sent.astype(BF)
        deliver(grads_out, grads_in, grads_s, grads_r, p)

    loop(0, half, give)

    terms = []
    for q in range(comps):
        acc = jnp.sum(blur[q, :, 128 : 128 + width].astype(F32) * back[q], axis=0, keepdims=True)
        gain = jnp.full((1, 1), amps[q], F32)
        terms.append(jnp.sum(acc, axis=1, keepdims=True) / (gain * gain * pixels))
    shift = jnp.sum(adj[...] * dot(slope_t, fet[...].astype(BF)), axis=0, keepdims=True)
    terms.append(jnp.sum(shift, axis=1, keepdims=True) / pixels)

    line = iota((8, 128), 0)
    card = jnp.where(line == 5, expo.astype(F32), 0.0)
    for q, term in enumerate(terms):
        card = jnp.where(line == q, jnp.broadcast_to(term, (8, 128)), card)
    card_out[...] = card
    cards[band] = card

    def swap(k, here):
        to = lax.rem(band + k, nband)
        return pltpu.make_async_remote_copy(
            src_ref=card_out,
            dst_ref=cards.at[band] if here else cards.at[to],
            send_sem=cards_s.at[to],
            recv_sem=cards_r.at[band] if here else cards_r.at[to],
            device_id={"band": to},
            device_id_type=MESH,
        )

    loop(1, nband, lambda k: swap(k, True).start())

    loop(half, tiles, give)

    loop(1, nband, lambda k: swap(k, False).wait_recv())
    expos = summed_ref.shape[1]
    column = iota((8, expos), 1).astype(F32)
    part = jnp.zeros((8, expos), F32)
    for b in range(nband):
        block = jnp.concatenate([cards[b]] * (expos // 128), axis=1)
        part = part + jnp.where(column == block[5:6, :], block, 0.0)
    part_out[...] = part
    part_in[me] = part

    def tell(k, here):
        p = lax.rem(me + k, tiles)
        return pltpu.make_async_remote_copy(
            src_ref=part_out,
            dst_ref=part_in.at[me] if here else part_in.at[p],
            send_sem=part_s.at[p],
            recv_sem=part_r.at[me] if here else part_r.at[p],
            device_id={"tile": p},
            device_id_type=MESH,
        )

    loop(1, tiles, lambda k: tell(k, True).start())

    total[...] = jnp.zeros_like(total)

    def collect(step):
        p = ahead(step)
        receive(grads_out, grads_in, grads_s, grads_r, p)
        chosen = picks[p] if keep else pick(p)
        total[...] += lax.dot_general(chosen, grads_in[p], NT, preferred_element_type=F32)

    loop(0, tiles, collect)

    loop(1, tiles, lambda k: tell(k, False).wait_recv())
    summed = lax.fori_loop(0, tiles, lambda t, acc: acc + part_in[t], jnp.zeros((8, expos), F32))
    summed_ref[...] = summed[: comps + 1]

    def settle(k):
        p = lax.rem(me + k, tiles)
        push(req_out, req_in, req_s, req_r, p).wait_send()
        push(rows_out, rows_in, rows_s, rows_r, p).wait_send()
        push(grads_out, grads_in, grads_s, grads_r, p).wait_send()
        tell(k, True).wait_send()

    loop(1, tiles, settle)
    loop(1, nband, lambda k: swap(k, True).wait_send())


def body(
    sky_model,
    observed,
    row_weight,
    foot_owner,
    foot_local,
    row_offset,
    exposure_of,
    amplitude,
    subpixel_shift,
    column_profile,
    row_profile,
):
    tiles = lax.axis_size("tile")
    nband = lax.axis_size("band")
    segs, rows = sky_model.shape[1:]
    width = observed.shape[2]
    comps, expos = amplitude.shape
    taps = column_profile.shape[2]
    cap = 2 * width // tiles
    vmem = pl.BlockSpec(memory_space=pltpu.VMEM)
    smem = pl.BlockSpec(memory_space=pltpu.SMEM)
    hbm = pl.BlockSpec(memory_space=pltpu.HBM)
    dma = pltpu.SemaphoreType.DMA
    grad, params = pl.pallas_call(
        functools.partial(kernel, tiles, nband, cap),
        out_shape=(
            jax.ShapeDtypeStruct((segs, rows), F32),
            jax.ShapeDtypeStruct((comps + 1, expos), F32),
        ),
        in_specs=[vmem, vmem, vmem, smem, smem, smem, smem, hbm, hbm, hbm, hbm],
        out_specs=(vmem, vmem),
        scratch_shapes=[
            pltpu.VMEM((segs, rows), BF),
            pltpu.VMEM((rows, segs), BF),
            pltpu.VMEM((width, rows), BF),
            pltpu.VMEM((taps, comps, expos), F32),
            pltpu.VMEM((taps, comps, expos), F32),
            pltpu.VMEM((tiles, cap, width), BF),
            pltpu.VMEM((tiles, segs, cap) if cap >= 128 else (16, 128), BF),
            pltpu.VMEM((tiles, 1, cap), F32),
            pltpu.VMEM((tiles, 1, cap), F32),
            pltpu.VMEM((tiles, rows, cap), BF),
            pltpu.VMEM((tiles, rows, cap), BF),
            pltpu.VMEM((tiles, rows, cap), BF),
            pltpu.VMEM((tiles, rows, cap), BF),
            pltpu.VMEM((8, 128), F32),
            pltpu.VMEM((nband, 8, 128), F32),
            pltpu.VMEM((8, expos), F32),
            pltpu.VMEM((tiles, 8, expos), F32),
            pltpu.VMEM((rows, width), F32),
            pltpu.VMEM((rows, width), BF),
            pltpu.VMEM((4, comps, 8, 256), F32),
            pltpu.VMEM((comps, rows, width + 256), BF),
            pltpu.VMEM((comps, 512, 256), BF),
            pltpu.VMEM((comps, 512, 256), BF),
            pltpu.VMEM((comps, rows, rows), BF),
            pltpu.VMEM((comps, rows, rows), BF),
            pltpu.VMEM((rows, width), BF),
            pltpu.VMEM((rows, width + 256), BF),
            pltpu.VMEM((comps, rows, width), F32),
            pltpu.VMEM((rows, width), F32),
            pltpu.VMEM((rows, width), BF),
            dma((4,)),
        ]
        + [dma((tiles,))] * 6
        + [dma((nband,))] * 2
        + [dma((tiles,))] * 2,
        compiler_params=pltpu.CompilerParams(
            collective_id=0, has_side_effects=True, vmem_limit_bytes=60 * 1024 * 1024
        ),
    )(
        foot_owner.reshape(1, width),
        foot_local.reshape(1, width),
        row_weight.reshape(1, rows),
        row_offset,
        exposure_of,
        amplitude,
        subpixel_shift,
        sky_model[0],
        observed[0, 0],
        column_profile.transpose(2, 1, 0),
        row_profile.transpose(2, 1, 0),
    )
    return (grad[None], params)


def solution(mesh):
    placed = (
        P("band", "tile", None),
        P("band", "tile", None, None),
        P("band", "tile", None),
        P("band", "tile", None, None),
        P("band", "tile", None),
        P("band", "tile"),
        P("band", "tile"),
        P(),
        P(),
        P(),
        P(),
    )
    return jax.shard_map(
        body, mesh=mesh, in_specs=placed, out_specs=(P("band", "tile", None), P()), check_vma=False
    )
```

```python
import functools

import jax
import jax.numpy as jnp
from jax import lax
from jax.experimental import pallas as pl
from jax.experimental.pallas import tpu as pltpu
from jax.sharding import PartitionSpec as P

MESH = pl.DeviceIdType.MESH
BF = jnp.bfloat16
F32 = jnp.float32
TN = (((0,), (0,)), ((), ()))
NT = (((1,), (1,)), ((), ()))


def iota(shape, dim):
    return lax.broadcasted_iota(jnp.int32, shape, dim)


def dot(a, b):
    return jnp.dot(a, b, preferred_element_type=F32)


def onehot(hit):
    return jnp.where(hit, 1.0, 0.0).astype(BF)


def spread(ref, expo):
    taps, comps, expos = ref.shape
    named = iota((comps, expos), 1) == expo
    lane = iota((comps, 256), 1) - (128 - taps // 2)
    straight = mirrored = jnp.zeros((comps, 256), F32)
    for t in range(taps):
        tap = jnp.sum(jnp.where(named, ref[t], 0.0), axis=1, keepdims=True)
        straight = jnp.where(lane == t, tap, straight)
        mirrored = jnp.where(lane == taps - 1 - t, tap, mirrored)
    return straight.astype(BF).astype(F32), mirrored.astype(BF).astype(F32)


def bands(base):
    x = jnp.concatenate([base] * 16, axis=0)
    row = iota(x.shape, 0)
    for bit in range(7):
        x = jnp.where((row & (1 << bit)) != 0, pltpu.roll(x, 1 << bit, 1), x)
    return x


def kernel(
    tiles,
    nband,
    cap,
    offset_ref,
    expo_ref,
    owner_hbm,
    local_hbm,
    weight_hbm,
    amp_hbm,
    frac_hbm,
    sky_hbm,
    obs_hbm,
    col_hbm,
    rowp_hbm,
    total,
    summed_ref,
    owner_ref,
    local_ref,
    weight_ref,
    amp_ref,
    frac_ref,
    sky,
    sky_t,
    obs,
    colp,
    rowp,
    hits,
    picks,
    req_out,
    req_in,
    rows_out,
    rows_in,
    grads_out,
    grads_in,
    card_out,
    cards,
    part_out,
    part_in,
    fet,
    resam,
    base,
    blur,
    fwd,
    bwd,
    tall,
    tall_t,
    obs_t,
    resid,
    back,
    adj,
    seg_grad,
    load_sem,
    req_s,
    req_r,
    rows_s,
    rows_r,
    grads_s,
    grads_r,
    cards_s,
    cards_r,
    part_s,
    part_r,
):
    me = lax.axis_index("tile")
    band = lax.axis_index("band")
    segs, rows = sky.shape
    width = obs.shape[0]
    comps = blur.shape[0]
    pixels = width * rows
    nblk = width // 256

    loads = [
        pltpu.make_async_copy(src, dst, load_sem.at[i])
        for i, (src, dst) in enumerate(
            (
                (owner_hbm, owner_ref),
                (local_hbm, local_ref),
                (sky_hbm, sky),
                (obs_hbm, obs),
                (col_hbm, colp),
                (rowp_hbm, rowp),
                (weight_hbm, weight_ref),
                (amp_hbm, amp_ref),
                (frac_hbm, frac_ref),
            )
        )
    ]
    for load in loads:
        load.start()

    barrier = pltpu.get_barrier_semaphore()

    def loop(low, high, work):
        lax.fori_loop(low, high, lambda k, c: (work(k), c)[1], 0)

    loop(
        1,
        tiles,
        lambda k: pl.semaphore_signal(
            barrier, inc=1, device_id={"tile": lax.rem(me + k, tiles)}, device_id_type=MESH
        ),
    )
    loop(
        1,
        nband,
        lambda k: pl.semaphore_signal(
            barrier, inc=1, device_id={"band": lax.rem(band + k, nband)}, device_id_type=MESH
        ),
    )

    def after(step):
        return lax.rem(me + 1 + step, tiles)

    def ahead(step):
        return lax.rem(me + 2 * tiles - 1 - step, tiles)

    def push(src, dst, send, recv, p):
        return pltpu.make_async_remote_copy(
            src_ref=src.at[p],
            dst_ref=dst.at[me],
            send_sem=send.at[p],
            recv_sem=recv.at[me],
            device_id={"tile": p},
            device_id_type=MESH,
        )

    def arrival(src, dst, send, recv, p):
        return pltpu.make_async_remote_copy(
            src_ref=src.at[p],
            dst_ref=dst.at[p],
            send_sem=send.at[p],
            recv_sem=recv.at[p],
            device_id={"tile": p},
            device_id_type=MESH,
        )

    def deliver(src, dst, send, recv, p):
        @pl.when(p != me)
        def _():
            push(src, dst, send, recv, p).start()

        @pl.when(p == me)
        def _():
            dst[me] = src[me]

    def receive(src, dst, send, recv, p):
        @pl.when(p != me)
        def _():
            arrival(src, dst, send, recv, p).wait_recv()

    loads[0].wait()
    loads[1].wait()
    owner = owner_ref[...]
    member = jnp.where(iota((tiles, width), 0) == owner, 1.0, 0.0)
    pieces = [member[:, b * 128 : (b + 1) * 128] for b in range(width // 128)]
    above = onehot(iota((128, 128), 0) < iota((128, 128), 1))
    prefix = dot(jnp.concatenate(pieces, axis=0).astype(BF), above)
    run = jnp.zeros((tiles, 1), F32)
    ranks = []
    for b, piece in enumerate(pieces):
        earlier = prefix[b * tiles : (b + 1) * tiles] + run
        ranks.append(jnp.sum(piece * earlier, axis=0, keepdims=True))
        run = run + jnp.sum(piece, axis=1, keepdims=True)
    slot = owner * cap + jnp.concatenate(ranks, axis=1).astype(jnp.int32)
    wanted = local_ref[...] + 1
    which = iota((16, width), 0)
    digits = (
        jnp.where(which == 0, wanted >> 6, jnp.where(which == 1, wanted & 63, 0))
        .astype(F32)
        .astype(BF)
    )
    pl.semaphore_wait(barrier, tiles - 1 + nband - 1)

    def ask(step):
        p = after(step)
        hit = onehot(iota((cap, width), 0) + p * cap == slot)
        hits[p] = hit
        ids = lax.dot_general(digits, hit, NT, preferred_element_type=F32)
        req_out[p] = ids[0:1] * 64.0 + ids[1:2]
        deliver(req_out, req_in, req_s, req_r, p)

    loop(0, tiles, ask)
    loads[2].wait()
    for b in range(segs // 128):
        sky_t[:, b * 128 : (b + 1) * 128] = sky[b * 128 : (b + 1) * 128, :].T

    keep = cap >= 128

    def pick(p):
        return onehot(iota((segs, cap), 0) + 1 == req_in[p].astype(jnp.int32))

    def serve(step):
        p = ahead(step)
        receive(req_out, req_in, req_s, req_r, p)
        chosen = pick(p)
        if keep:
            picks[p] = chosen
        rows_out[p] = dot(sky_t[...], chosen).astype(BF)
        deliver(rows_out, rows_in, rows_s, rows_r, p)

    loop(0, tiles, serve)

    for load in loads[3:]:
        load.wait()
    expo = expo_ref[0, 0]
    offset = offset_ref[0, 0]
    amps = [amp_ref[q, expo] for q in range(comps)]
    for at, made in enumerate((*spread(colp, expo), *spread(rowp, expo))):
        for q in range(comps):
            base[at, q] = jnp.broadcast_to(made[q : q + 1], (8, 256))
    low = iota((128, 128), 1) < 64
    blank = jnp.zeros((128, 128), BF)

    def make_wide(at, wide):
        def work(q):
            made = bands(base[at, q])
            edge, mid = made[:, :128], made[:, 128:].astype(BF)
            left = jnp.where(low, 0.0, edge).astype(BF)
            right = jnp.where(low, edge, 0.0).astype(BF)
            for b, line in enumerate(((right, blank), (mid, right), (left, mid), (blank, left))):
                for h in range(2):
                    wide[q, b * 128 : (b + 1) * 128, h * 128 : (h + 1) * 128] = line[h]

        loop(0, comps, work)

    make_wide(1, fwd)
    make_wide(0, bwd)

    def make_tall(q):
        tall[q] = bands(base[2, q])[:, 128:].astype(BF)
        tall_t[q] = bands(base[3, q])[:, 128:].astype(BF)
        blur[q, :, :128] = blank
        blur[q, :, 128 + width :] = blank

    loop(0, comps, make_tall)
    resid[:, :128] = blank
    resid[:, 128 + width :] = blank
    for b in range(width // 128):
        obs_t[:, b * 128 : (b + 1) * 128] = obs[b * 128 : (b + 1) * 128, :].T
    heavy = jnp.broadcast_to(weight_ref[...], (128, 128)).T
    heavy = jnp.concatenate([heavy, heavy], axis=1)
    frac = jnp.full((128, 128), frac_ref[expo], F32)
    w_low = (1.0 - frac).astype(BF).astype(F32)
    w_high = frac.astype(BF).astype(F32)
    sub, lane = iota((128, 128), 0), iota((128, 128), 1)
    interp_t = (
        jnp.where(lane == sub + offset, w_low, 0.0)
        + jnp.where(lane == sub + offset + 1, w_high, 0.0)
    ).astype(BF)
    interp = (
        jnp.where(sub == lane + offset, w_low, 0.0)
        + jnp.where(sub == lane + offset + 1, w_high, 0.0)
    ).astype(BF)
    slope_t = (
        jnp.where(lane == sub + offset + 1, 1.0, 0.0) - jnp.where(lane == sub + offset, 1.0, 0.0)
    ).astype(BF)

    fet[...] = jnp.zeros_like(fet)

    def take(step):
        p = after(step)
        receive(rows_out, rows_in, rows_s, rows_r, p)
        fet[...] += dot(rows_in[p], hits[p])

    loop(0, tiles, take)

    resam[...] = dot(interp_t, fet[...].astype(BF)).astype(BF)

    tall_rows = jnp.concatenate([tall[q] for q in range(comps)], axis=0)
    for i in range(nblk):
        part = dot(tall_rows, resam[:, i * 256 : (i + 1) * 256])
        for q in range(comps):
            blur[q, :, 128 + i * 256 : 384 + i * 256] = (
                amps[q] * part[q * 128 : (q + 1) * 128]
            ).astype(BF)

    for i in range(nblk):
        model = None
        for q in range(comps):
            part = dot(blur[q, :, i * 256 : i * 256 + 512], fwd[q])
            model = part if model is None else model + part
        weighted = heavy * (model - obs_t[:, i * 256 : (i + 1) * 256].astype(F32))
        resid[:, 128 + i * 256 : 384 + i * 256] = weighted.astype(BF)
    tall_all = jnp.concatenate([tall_t[q] for q in range(comps)], axis=1)
    for i in range(nblk):
        left = resid[:, i * 256 : i * 256 + 512]
        stack = []
        for q in range(comps):
            part = amps[q] * dot(left, bwd[q])
            back[q, :, i * 256 : (i + 1) * 256] = part
            stack.append(part.astype(BF))
        adjoint = dot(tall_all, jnp.concatenate(stack, axis=0))
        adj[:, i * 256 : (i + 1) * 256] = adjoint
        seg_grad[i * 256 : (i + 1) * 256, :] = dot(interp, adjoint.astype(BF)).T.astype(BF)

    def give(step):
        p = after(step)
        grads_out[p] = dot(hits[p], seg_grad[...]).astype(BF)
        deliver(grads_out, grads_in, grads_s, grads_r, p)

    loop(0, tiles, give)

    terms = []
    for q in range(comps):
        acc = jnp.sum(blur[q, :, 128 : 128 + width].astype(F32) * back[q], axis=0, keepdims=True)
        gain = jnp.full((1, 1), amps[q], F32)
        terms.append(jnp.sum(acc, axis=1, keepdims=True) / (gain * gain * pixels))
    shift = jnp.sum(adj[...] * dot(slope_t, fet[...].astype(BF)), axis=0, keepdims=True)
    terms.append(jnp.sum(shift, axis=1, keepdims=True) / pixels)

    line = iota((8, 128), 0)
    card = jnp.where(line == 5, expo.astype(F32), 0.0)
    for q, term in enumerate(terms):
        card = jnp.where(line == q, jnp.broadcast_to(term, (8, 128)), card)
    card_out[...] = card
    cards[band] = card

    def swap(k, here):
        to = lax.rem(band + k, nband)
        return pltpu.make_async_remote_copy(
            src_ref=card_out,
            dst_ref=cards.at[band] if here else cards.at[to],
            send_sem=cards_s.at[to],
            recv_sem=cards_r.at[band] if here else cards_r.at[to],
            device_id={"band": to},
            device_id_type=MESH,
        )

    loop(1, nband, lambda k: swap(k, True).start())

    loop(1, nband, lambda k: swap(k, False).wait_recv())
    expos = summed_ref.shape[1]
    column = iota((8, expos), 1).astype(F32)
    part = jnp.zeros((8, expos), F32)
    for b in range(nband):
        block = jnp.concatenate([cards[b]] * (expos // 128), axis=1)
        part = part + jnp.where(column == block[5:6, :], block, 0.0)
    part_out[...] = part
    part_in[me] = part

    def tell(k, here):
        p = lax.rem(me + k, tiles)
        return pltpu.make_async_remote_copy(
            src_ref=part_out,
            dst_ref=part_in.at[me] if here else part_in.at[p],
            send_sem=part_s.at[p],
            recv_sem=part_r.at[me] if here else part_r.at[p],
            device_id={"tile": p},
            device_id_type=MESH,
        )

    loop(1, tiles, lambda k: tell(k, True).start())

    total[...] = jnp.zeros_like(total)

    def collect(step):
        p = ahead(step)
        receive(grads_out, grads_in, grads_s, grads_r, p)
        chosen = picks[p] if keep else pick(p)
        total[...] += dot(chosen, grads_in[p])

    loop(0, tiles, collect)

    loop(1, tiles, lambda k: tell(k, False).wait_recv())
    summed = lax.fori_loop(0, tiles, lambda t, acc: acc + part_in[t], jnp.zeros((8, expos), F32))
    summed_ref[...] = summed[: comps + 1]

    def settle(k):
        p = lax.rem(me + k, tiles)
        push(req_out, req_in, req_s, req_r, p).wait_send()
        push(rows_out, rows_in, rows_s, rows_r, p).wait_send()
        push(grads_out, grads_in, grads_s, grads_r, p).wait_send()
        tell(k, True).wait_send()

    loop(1, tiles, settle)
    loop(1, nband, lambda k: swap(k, True).wait_send())


def body(
    sky_model,
    observed,
    row_weight,
    foot_owner,
    foot_local,
    row_offset,
    exposure_of,
    amplitude,
    subpixel_shift,
    column_profile,
    row_profile,
):
    tiles = lax.axis_size("tile")
    nband = lax.axis_size("band")
    segs, rows = sky_model.shape[1:]
    width = observed.shape[2]
    comps, expos = amplitude.shape
    taps = column_profile.shape[2]
    cap = 2 * width // tiles
    vmem = pl.BlockSpec(memory_space=pltpu.VMEM)
    smem = pl.BlockSpec(memory_space=pltpu.SMEM)
    hbm = pl.BlockSpec(memory_space=pltpu.HBM)
    dma = pltpu.SemaphoreType.DMA
    grad, params = pl.pallas_call(
        functools.partial(kernel, tiles, nband, cap),
        out_shape=(
            jax.ShapeDtypeStruct((segs, rows), F32),
            jax.ShapeDtypeStruct((comps + 1, expos), F32),
        ),
        in_specs=[smem] * 2 + [hbm] * 9,
        out_specs=(vmem, vmem),
        scratch_shapes=[
            pltpu.VMEM((1, width), jnp.int32),
            pltpu.VMEM((1, width), jnp.int32),
            pltpu.VMEM((1, rows), F32),
            pltpu.SMEM((comps, expos), F32),
            pltpu.SMEM((expos,), F32),
            pltpu.VMEM((segs, rows), BF),
            pltpu.VMEM((rows, segs), BF),
            pltpu.VMEM((width, rows), BF),
            pltpu.VMEM((taps, comps, expos), F32),
            pltpu.VMEM((taps, comps, expos), F32),
            pltpu.VMEM((tiles, cap, width), BF),
            pltpu.VMEM((tiles, segs, cap) if cap >= 128 else (16, 128), BF),
            pltpu.VMEM((tiles, 1, cap), F32),
            pltpu.VMEM((tiles, 1, cap), F32),
            pltpu.VMEM((tiles, rows, cap), BF),
            pltpu.VMEM((tiles, rows, cap), BF),
            pltpu.VMEM((tiles, cap, rows), BF),
            pltpu.VMEM((tiles, cap, rows), BF),
            pltpu.VMEM((8, 128), F32),
            pltpu.VMEM((nband, 8, 128), F32),
            pltpu.VMEM((8, expos), F32),
            pltpu.VMEM((tiles, 8, expos), F32),
            pltpu.VMEM((rows, width), F32),
            pltpu.VMEM((rows, width), BF),
            pltpu.VMEM((4, comps, 8, 256), F32),
            pltpu.VMEM((comps, rows, width + 256), BF),
            pltpu.VMEM((comps, 512, 256), BF),
            pltpu.VMEM((comps, 512, 256), BF),
            pltpu.VMEM((comps, rows, rows), BF),
            pltpu.VMEM((comps, rows, rows), BF),
            pltpu.VMEM((rows, width), BF),
            pltpu.VMEM((rows, width + 256), BF),
            pltpu.VMEM((comps, rows, width), F32),
            pltpu.VMEM((rows, width), F32),
            pltpu.VMEM((width, rows), BF),
            dma((9,)),
        ]
        + [dma((tiles,))] * 6
        + [dma((nband,))] * 2
        + [dma((tiles,))] * 2,
        compiler_params=pltpu.CompilerParams(
            collective_id=0, has_side_effects=True, vmem_limit_bytes=60 * 1024 * 1024
        ),
    )(
        row_offset,
        exposure_of,
        foot_owner.reshape(1, width),
        foot_local.reshape(1, width),
        row_weight.reshape(1, rows),
        amplitude,
        subpixel_shift,
        sky_model[0],
        observed[0, 0],
        column_profile.transpose(2, 1, 0),
        row_profile.transpose(2, 1, 0),
    )
    return (grad[None], params)


def solution(mesh):
    placed = (
        P("band", "tile", None),
        P("band", "tile", None, None),
        P("band", "tile", None),
        P("band", "tile", None, None),
        P("band", "tile", None),
        P("band", "tile"),
        P("band", "tile"),
        P(),
        P(),
        P(),
        P(),
    )
    return jax.shard_map(
        body, mesh=mesh, in_specs=placed, out_specs=(P("band", "tile", None), P()), check_vma=False
    )
```

```python
import functools

import jax
import jax.numpy as jnp
from jax import lax
from jax.experimental import pallas as pl
from jax.experimental.pallas import tpu as pltpu
from jax.sharding import PartitionSpec as P

MESH = pl.DeviceIdType.MESH
BF = jnp.bfloat16
F32 = jnp.float32
TN = (((0,), (0,)), ((), ()))
NT = (((1,), (1,)), ((), ()))


def iota(shape, dim):
    return lax.broadcasted_iota(jnp.int32, shape, dim)


def dot(a, b):
    return jnp.dot(a, b, preferred_element_type=F32)


def onehot(hit):
    return jnp.where(hit, 1.0, 0.0).astype(BF)


def spread(ref, expo):
    taps, comps, expos = ref.shape
    named = iota((comps, expos), 1) == expo
    lane = iota((comps, 256), 1) - (128 - taps // 2)
    straight = mirrored = jnp.zeros((comps, 256), F32)
    for t in range(taps):
        tap = jnp.sum(jnp.where(named, ref[t], 0.0), axis=1, keepdims=True)
        straight = jnp.where(lane == t, tap, straight)
        mirrored = jnp.where(lane == taps - 1 - t, tap, mirrored)
    return straight.astype(BF).astype(F32), mirrored.astype(BF).astype(F32)


def bands(base):
    x = jnp.concatenate([base] * 16, axis=0)
    row = iota(x.shape, 0)
    for bit in range(7):
        x = jnp.where((row & (1 << bit)) != 0, pltpu.roll(x, 1 << bit, 1), x)
    return x


def kernel(
    tiles,
    nband,
    cap,
    offset_ref,
    expo_ref,
    owner_hbm,
    local_hbm,
    weight_hbm,
    amp_hbm,
    frac_hbm,
    sky_hbm,
    obs_hbm,
    col_hbm,
    rowp_hbm,
    grad_hbm,
    summed_ref,
    owner_ref,
    local_ref,
    weight_ref,
    amp_ref,
    frac_ref,
    sky,
    sky_t,
    obs,
    colp,
    rowp,
    hits,
    picks,
    req_out,
    req_in,
    rows_out,
    rows_in,
    grads_out,
    grads_in,
    card_out,
    cards,
    part_out,
    part_in,
    fet,
    resam,
    base,
    blur,
    fwd,
    bwd,
    tall,
    tall_t,
    obs_t,
    resid,
    back,
    adj,
    seg_grad,
    total,
    load_sem,
    store_sem,
    req_s,
    req_r,
    rows_s,
    rows_r,
    grads_s,
    grads_r,
    cards_s,
    cards_r,
    part_s,
    part_r,
):
    me = lax.axis_index("tile")
    band = lax.axis_index("band")
    segs, rows = sky.shape
    width = obs.shape[0]
    comps = blur.shape[0]
    pixels = width * rows
    nblk = width // 256

    loads = [
        pltpu.make_async_copy(src, dst, load_sem.at[i])
        for i, (src, dst) in enumerate(
            (
                (owner_hbm, owner_ref),
                (local_hbm, local_ref),
                (sky_hbm, sky),
                (obs_hbm, obs),
                (col_hbm, colp),
                (rowp_hbm, rowp),
                (weight_hbm, weight_ref),
                (amp_hbm, amp_ref),
                (frac_hbm, frac_ref),
            )
        )
    ]
    for load in loads:
        load.start()

    barrier = pltpu.get_barrier_semaphore()

    def loop(low, high, work):
        lax.fori_loop(low, high, lambda k, c: (work(k), c)[1], 0)

    loop(
        1,
        tiles,
        lambda k: pl.semaphore_signal(
            barrier, inc=1, device_id={"tile": lax.rem(me + k, tiles)}, device_id_type=MESH
        ),
    )
    loop(
        1,
        nband,
        lambda k: pl.semaphore_signal(
            barrier, inc=1, device_id={"band": lax.rem(band + k, nband)}, device_id_type=MESH
        ),
    )

    def after(step):
        return lax.rem(me + 1 + step, tiles)

    def ahead(step):
        return lax.rem(me + 2 * tiles - 1 - step, tiles)

    def push(src, dst, send, recv, p):
        return pltpu.make_async_remote_copy(
            src_ref=src.at[p],
            dst_ref=dst.at[me],
            send_sem=send.at[p],
            recv_sem=recv.at[me],
            device_id={"tile": p},
            device_id_type=MESH,
        )

    def arrival(src, dst, send, recv, p):
        return pltpu.make_async_remote_copy(
            src_ref=src.at[p],
            dst_ref=dst.at[p],
            send_sem=send.at[p],
            recv_sem=recv.at[p],
            device_id={"tile": p},
            device_id_type=MESH,
        )

    def deliver(src, dst, send, recv, p):
        @pl.when(p != me)
        def _():
            push(src, dst, send, recv, p).start()

        @pl.when(p == me)
        def _():
            dst[me] = src[me]

    def receive(src, dst, send, recv, p):
        @pl.when(p != me)
        def _():
            arrival(src, dst, send, recv, p).wait_recv()

    loads[0].wait()
    loads[1].wait()
    owner = owner_ref[...]
    member = jnp.where(iota((tiles, width), 0) == owner, 1.0, 0.0)
    pieces = [member[:, b * 128 : (b + 1) * 128] for b in range(width // 128)]
    above = onehot(iota((128, 128), 0) < iota((128, 128), 1))
    prefix = dot(jnp.concatenate(pieces, axis=0).astype(BF), above)
    run = jnp.zeros((tiles, 1), F32)
    ranks = []
    for b, piece in enumerate(pieces):
        earlier = prefix[b * tiles : (b + 1) * tiles] + run
        ranks.append(jnp.sum(piece * earlier, axis=0, keepdims=True))
        run = run + jnp.sum(piece, axis=1, keepdims=True)
    slot = owner * cap + jnp.concatenate(ranks, axis=1).astype(jnp.int32)
    wanted = local_ref[...] + 1
    which = iota((16, width), 0)
    digits = (
        jnp.where(which == 0, wanted >> 6, jnp.where(which == 1, wanted & 63, 0))
        .astype(F32)
        .astype(BF)
    )
    pl.semaphore_wait(barrier, tiles - 1 + nband - 1)

    def ask(step):
        p = after(step)
        hit = onehot(iota((cap, width), 0) + p * cap == slot)
        hits[p] = hit
        ids = lax.dot_general(digits, hit, NT, preferred_element_type=F32)
        req_out[p] = ids[0:1] * 64.0 + ids[1:2]
        deliver(req_out, req_in, req_s, req_r, p)

    loop(0, tiles, ask)
    loads[2].wait()
    for b in range(segs // 128):
        sky_t[:, b * 128 : (b + 1) * 128] = sky[b * 128 : (b + 1) * 128, :].T

    keep = cap >= 128

    def pick(p):
        return onehot(iota((segs, cap), 0) + 1 == req_in[p].astype(jnp.int32))

    def serve(step):
        p = ahead(step)
        receive(req_out, req_in, req_s, req_r, p)
        chosen = pick(p)
        if keep:
            picks[p] = chosen
        rows_out[p] = dot(sky_t[...], chosen).astype(BF)
        deliver(rows_out, rows_in, rows_s, rows_r, p)

    loop(0, tiles, serve)

    for load in loads[3:]:
        load.wait()
    expo = expo_ref[0, 0]
    offset = offset_ref[0, 0]
    amps = [amp_ref[q, expo] for q in range(comps)]
    for at, made in enumerate((*spread(colp, expo), *spread(rowp, expo))):
        for q in range(comps):
            base[at, q] = jnp.broadcast_to(made[q : q + 1], (8, 256))
    low = iota((128, 128), 1) < 64
    blank = jnp.zeros((128, 128), BF)

    def make_wide(at, wide):
        def work(q):
            made = bands(base[at, q])
            edge, mid = made[:, :128], made[:, 128:].astype(BF)
            left = jnp.where(low, 0.0, edge).astype(BF)
            right = jnp.where(low, edge, 0.0).astype(BF)
            for b, line in enumerate(((right, blank), (mid, right), (left, mid), (blank, left))):
                for h in range(2):
                    wide[q, b * 128 : (b + 1) * 128, h * 128 : (h + 1) * 128] = line[h]

        loop(0, comps, work)

    make_wide(1, fwd)
    make_wide(0, bwd)

    def make_tall(q):
        tall[q] = bands(base[2, q])[:, 128:].astype(BF)
        tall_t[q] = bands(base[3, q])[:, 128:].astype(BF)
        blur[q, :, :128] = blank
        blur[q, :, 128 + width :] = blank

    loop(0, comps, make_tall)
    resid[:, :128] = blank
    resid[:, 128 + width :] = blank
    for b in range(width // 128):
        obs_t[:, b * 128 : (b + 1) * 128] = obs[b * 128 : (b + 1) * 128, :].T
    heavy = jnp.broadcast_to(weight_ref[...], (128, 128)).T
    heavy = jnp.concatenate([heavy, heavy], axis=1)
    frac = jnp.full((128, 128), frac_ref[expo], F32)
    w_low = (1.0 - frac).astype(BF).astype(F32)
    w_high = frac.astype(BF).astype(F32)
    sub, lane = iota((128, 128), 0), iota((128, 128), 1)
    interp_t = (
        jnp.where(lane == sub + offset, w_low, 0.0)
        + jnp.where(lane == sub + offset + 1, w_high, 0.0)
    ).astype(BF)
    interp = (
        jnp.where(sub == lane + offset, w_low, 0.0)
        + jnp.where(sub == lane + offset + 1, w_high, 0.0)
    ).astype(BF)
    slope_t = (
        jnp.where(lane == sub + offset + 1, 1.0, 0.0) - jnp.where(lane == sub + offset, 1.0, 0.0)
    ).astype(BF)

    fet[...] = jnp.zeros_like(fet)

    def take(step):
        p = lax.rem(me + step, tiles)
        receive(rows_out, rows_in, rows_s, rows_r, p)
        fet[...] += dot(rows_in[p], hits[p])

    loop(0, tiles, take)

    resam[...] = dot(interp_t, fet[...].astype(BF)).astype(BF)

    tall_rows = jnp.concatenate([tall[q] for q in range(comps)], axis=0)
    for i in range(nblk):
        part = dot(tall_rows, resam[:, i * 256 : (i + 1) * 256])
        for q in range(comps):
            blur[q, :, 128 + i * 256 : 384 + i * 256] = (
                amps[q] * part[q * 128 : (q + 1) * 128]
            ).astype(BF)

    for i in range(nblk):
        model = None
        for q in range(comps):
            part = dot(blur[q, :, i * 256 : i * 256 + 512], fwd[q])
            model = part if model is None else model + part
        weighted = heavy * (model - obs_t[:, i * 256 : (i + 1) * 256].astype(F32))
        resid[:, 128 + i * 256 : 384 + i * 256] = weighted.astype(BF)
    tall_all = jnp.concatenate([tall_t[q] for q in range(comps)], axis=1)
    for i in range(nblk):
        left = resid[:, i * 256 : i * 256 + 512]
        stack = []
        for q in range(comps):
            part = amps[q] * dot(left, bwd[q])
            back[q, :, i * 256 : (i + 1) * 256] = part
            stack.append(part.astype(BF))
        adjoint = dot(tall_all, jnp.concatenate(stack, axis=0))
        adj[:, i * 256 : (i + 1) * 256] = adjoint
        seg_grad[i * 256 : (i + 1) * 256, :] = dot(interp, adjoint.astype(BF)).T.astype(BF)

    def give(step):
        p = after(step)
        grads_out[p] = dot(hits[p], seg_grad[...]).astype(BF)
        deliver(grads_out, grads_in, grads_s, grads_r, p)

    loop(0, tiles, give)

    terms = []
    for q in range(comps):
        acc = jnp.sum(blur[q, :, 128 : 128 + width].astype(F32) * back[q], axis=0, keepdims=True)
        gain = jnp.full((1, 1), amps[q], F32)
        terms.append(jnp.sum(acc, axis=1, keepdims=True) / (gain * gain * pixels))
    shift = jnp.sum(adj[...] * dot(slope_t, fet[...].astype(BF)), axis=0, keepdims=True)
    terms.append(jnp.sum(shift, axis=1, keepdims=True) / pixels)

    line = iota((8, 128), 0)
    card = jnp.where(line == 5, expo.astype(F32), 0.0)
    for q, term in enumerate(terms):
        card = jnp.where(line == q, jnp.broadcast_to(term, (8, 128)), card)
    card_out[...] = card
    cards[band] = card

    def swap(k, here):
        to = lax.rem(band + k, nband)
        return pltpu.make_async_remote_copy(
            src_ref=card_out,
            dst_ref=cards.at[band] if here else cards.at[to],
            send_sem=cards_s.at[to],
            recv_sem=cards_r.at[band] if here else cards_r.at[to],
            device_id={"band": to},
            device_id_type=MESH,
        )

    loop(1, nband, lambda k: swap(k, True).start())

    loop(1, nband, lambda k: swap(k, False).wait_recv())
    expos = summed_ref.shape[1]
    column = iota((8, expos), 1).astype(F32)
    part = jnp.zeros((8, expos), F32)
    for b in range(nband):
        block = jnp.concatenate([cards[b]] * (expos // 128), axis=1)
        part = part + jnp.where(column == block[5:6, :], block, 0.0)
    part_out[...] = part
    part_in[me] = part

    def tell(k, here):
        p = lax.rem(me + k, tiles)
        return pltpu.make_async_remote_copy(
            src_ref=part_out,
            dst_ref=part_in.at[me] if here else part_in.at[p],
            send_sem=part_s.at[p],
            recv_sem=part_r.at[me] if here else part_r.at[p],
            device_id={"tile": p},
            device_id_type=MESH,
        )

    loop(1, tiles, lambda k: tell(k, True).start())

    total[...] = jnp.zeros_like(total)

    def collect(step):
        p = lax.rem(me + tiles - step, tiles)
        receive(grads_out, grads_in, grads_s, grads_r, p)
        chosen = picks[p] if keep else pick(p)
        total[...] += dot(chosen, grads_in[p])

    loop(0, tiles - 1, collect)
    last = lax.rem(me + 1, tiles)
    arrival(grads_out, grads_in, grads_s, grads_r, last).wait_recv()
    chosen = None if keep else pick(last)
    stores = []
    size = segs // 4
    for i in range(4):
        at = slice(i * size, (i + 1) * size)
        total[at, :] += dot(picks[last, at, :] if keep else chosen[at], grads_in[last])
        stores.append(
            pltpu.make_async_copy(
                total.at[pl.ds(i * size, size)], grad_hbm.at[pl.ds(i * size, size)], store_sem.at[i]
            )
        )
        stores[-1].start()

    loop(1, tiles, lambda k: tell(k, False).wait_recv())
    summed = lax.fori_loop(0, tiles, lambda t, acc: acc + part_in[t], jnp.zeros((8, expos), F32))
    summed_ref[...] = summed[: comps + 1]

    def settle(k):
        p = lax.rem(me + k, tiles)
        push(req_out, req_in, req_s, req_r, p).wait_send()
        push(rows_out, rows_in, rows_s, rows_r, p).wait_send()
        push(grads_out, grads_in, grads_s, grads_r, p).wait_send()
        tell(k, True).wait_send()

    loop(1, tiles, settle)
    loop(1, nband, lambda k: swap(k, True).wait_send())
    for store in stores:
        store.wait()


def body(
    sky_model,
    observed,
    row_weight,
    foot_owner,
    foot_local,
    row_offset,
    exposure_of,
    amplitude,
    subpixel_shift,
    column_profile,
    row_profile,
):
    tiles = lax.axis_size("tile")
    nband = lax.axis_size("band")
    segs, rows = sky_model.shape[1:]
    width = observed.shape[2]
    comps, expos = amplitude.shape
    taps = column_profile.shape[2]
    cap = 2 * width // tiles
    vmem = pl.BlockSpec(memory_space=pltpu.VMEM)
    smem = pl.BlockSpec(memory_space=pltpu.SMEM)
    hbm = pl.BlockSpec(memory_space=pltpu.HBM)
    dma = pltpu.SemaphoreType.DMA
    grad, params = pl.pallas_call(
        functools.partial(kernel, tiles, nband, cap),
        out_shape=(
            jax.ShapeDtypeStruct((segs, rows), F32),
            jax.ShapeDtypeStruct((comps + 1, expos), F32),
        ),
        in_specs=[smem] * 2 + [hbm] * 9,
        out_specs=(hbm, vmem),
        scratch_shapes=[
            pltpu.VMEM((1, width), jnp.int32),
            pltpu.VMEM((1, width), jnp.int32),
            pltpu.VMEM((1, rows), F32),
            pltpu.SMEM((comps, expos), F32),
            pltpu.SMEM((expos,), F32),
            pltpu.VMEM((segs, rows), BF),
            pltpu.VMEM((rows, segs), BF),
            pltpu.VMEM((width, rows), BF),
            pltpu.VMEM((taps, comps, expos), F32),
            pltpu.VMEM((taps, comps, expos), F32),
            pltpu.VMEM((tiles, cap, width), BF),
            pltpu.VMEM((tiles, segs, cap) if cap >= 128 else (16, 128), BF),
            pltpu.VMEM((tiles, 1, cap), F32),
            pltpu.VMEM((tiles, 1, cap), F32),
            pltpu.VMEM((tiles, rows, cap), BF),
            pltpu.VMEM((tiles, rows, cap), BF),
            pltpu.VMEM((tiles, cap, rows), BF),
            pltpu.VMEM((tiles, cap, rows), BF),
            pltpu.VMEM((8, 128), F32),
            pltpu.VMEM((nband, 8, 128), F32),
            pltpu.VMEM((8, expos), F32),
            pltpu.VMEM((tiles, 8, expos), F32),
            pltpu.VMEM((rows, width), F32),
            pltpu.VMEM((rows, width), BF),
            pltpu.VMEM((4, comps, 8, 256), F32),
            pltpu.VMEM((comps, rows, width + 256), BF),
            pltpu.VMEM((comps, 512, 256), BF),
            pltpu.VMEM((comps, 512, 256), BF),
            pltpu.VMEM((comps, rows, rows), BF),
            pltpu.VMEM((comps, rows, rows), BF),
            pltpu.VMEM((rows, width), BF),
            pltpu.VMEM((rows, width + 256), BF),
            pltpu.VMEM((comps, rows, width), F32),
            pltpu.VMEM((rows, width), F32),
            pltpu.VMEM((width, rows), BF),
            pltpu.VMEM((segs, rows), F32),
            dma((9,)),
            dma((4,)),
        ]
        + [dma((tiles,))] * 6
        + [dma((nband,))] * 2
        + [dma((tiles,))] * 2,
        compiler_params=pltpu.CompilerParams(
            collective_id=0, has_side_effects=True, vmem_limit_bytes=60 * 1024 * 1024
        ),
    )(
        row_offset,
        exposure_of,
        foot_owner.reshape(1, width),
        foot_local.reshape(1, width),
        row_weight.reshape(1, rows),
        amplitude,
        subpixel_shift,
        sky_model[0],
        observed[0, 0],
        column_profile.transpose(2, 1, 0),
        row_profile.transpose(2, 1, 0),
    )
    return (grad[None], params)


def solution(mesh):
    placed = (
        P("band", "tile", None),
        P("band", "tile", None, None),
        P("band", "tile", None),
        P("band", "tile", None, None),
        P("band", "tile", None),
        P("band", "tile"),
        P("band", "tile"),
        P(),
        P(),
        P(),
        P(),
    )
    return jax.shard_map(
        body, mesh=mesh, in_specs=placed, out_specs=(P("band", "tile", None), P()), check_vma=False
    )
```
